128 devices in a mesh: blk: 16 (over x, y_hi, core), tp: 8 (over y_lo, z).
Axes of the slice: x: 4, y: 4 (y_hi: 2, y_lo: 2; y = y_hi * 2 + y_lo), z: 4, core: 2. Of those that a mesh axis runs over, the one named last changes fastest.
Arguments:
- tokens: bfloat16 [4096, 8192], P('blk', 'tp'), may hold values from -6 to 6
- w_query: bfloat16 [8192, 4096], P(None, 'tp'), may hold values from -0.0625 to 0.0625
- w_key: bfloat16 [8192, 1024], P(None, 'tp'), may hold values from -0.0625 to 0.0625
- w_value: bfloat16 [8192, 1024], P(None, 'tp'), may hold values from -0.0625 to 0.0625
- w_out: bfloat16 [4096, 8192], P('tp'), may hold values from -3.5 to 3.5
- pool_keys: bfloat16 [32768, 8, 128], P('blk', 'tp'), may hold values from -175 to 175
- pool_values: bfloat16 [32768, 8, 128], P('blk', 'tp'), may hold values from -6 to 6
- block_lists: int32 [32, 8], P('blk'), may hold values from 0 to 63, all different within a row
- offsets: int32 [32], P('blk'), may hold values from 0 to 2047
Outputs:
- attended: bfloat16 [4096, 8192], P(('blk', 'tp'))
The draws below stay inside these ranges and needn't reach their ends.
Inputs may be any that keep to these rules, and one draw needn't show every extreme that they name: `block_lists`: each session's row names 8 different persona blocks, and every block is named by some session.
All inputs are finite; a program needn't handle non-finite values.
Results may differ from the reference program's by a relative error of at most 0.02.
Values may be sent and summed in bfloat16 or wider, within the bound.
No kernel may reach another device: no remote copies, remote signals or barrier semaphores. Data moves between devices by JAX's collectives and lax.ppermute only.
A program may use at most 128 MiB of HBM per device.

```python
import math
import jax
import jax.numpy as jnp
from jax import lax

D = 8192
QH = 32
KVH = 8
HD = 128
TURN = 128
BLOCK = 512
NSEL = 8
SESSIONS = 32
TOKENS = 4096
NBLOCKS = 64
POOL = 32768


def draw_pool_keys(key, part):
    key = jax.random.fold_in(key, 7)
    shape = (POOL, KVH, HD)
    return jnp.clip(jax.random.normal(key, shape, jnp.float32), -5.0, 5.0).astype(jnp.bfloat16)


def with_ends(entries, own_key, least, high):
    longest = entries.shape.index(max(entries.shape))
    spots = []
    for shift in (0, 1):
        where = [jax.random.randint(jax.random.fold_in(own_key, axis), (), 0, length) for axis, length in enumerate(entries.shape)]
        where[longest] = (where[longest] + shift) % entries.shape[longest]
        spots.append(tuple(where))
    return entries.at[spots[0]].set(least).at[spots[1]].set(high)


def shard_levels(rng, shape, shards, low, top_value):
    loudness, own = 1.0, jax.random.fold_in(rng, 6)
    for axis_at, blocks in shards:
        heights = jnp.exp(jax.random.uniform(jax.random.fold_in(own, axis_at), (blocks,), jnp.float32, low / len(shards), top_value / len(shards)))
        loudness = loudness * jnp.repeat(heights, shape[axis_at] // blocks).reshape([-1 if axis == axis_at else 1 for axis in range(len(shape))])
    return loudness


def distinct(rng, rows, count, top, lift):
    ranking = jax.random.permutation(jax.random.fold_in(rng, 1), count)
    pull = ranking
    for power in range(3):
        pull = pull * pull // count
    pull = pull * lift // count
    chance = jax.random.randint(jax.random.fold_in(rng, 2), (rows, count), 0, 4096) + pull
    sure = jax.random.permutation(jax.random.fold_in(rng, 3), rows)[jnp.arange(count) % rows]
    chance = jnp.where(jnp.arange(rows)[:, None] == sure[None, :], 1 << 14, chance)
    priority = chance * count + jnp.arange(count)
    return lax.top_k(priority.astype(jnp.int32), top)[1].astype(jnp.int32)


def normal_values(key, dims, width, bound, split=(), held_as=jnp.bfloat16):
    entries = width * jax.random.normal(key, dims, jnp.float32)
    if split:
        entries = entries * shard_levels(key, dims, split, -0.22, 0.18)
    return jnp.clip(entries, -bound, bound).astype(held_as)


def setup_inputs(seed: int = 0) -> dict:
    arg_keys = jax.random.split(jax.random.key(seed), 10)
    tokens = normal_values(arg_keys[0], (TOKENS, D), 1.0, 6.0, ((0, 16), (1, 8)))
    w_query = normal_values(arg_keys[1], (D, QH * HD), D ** -0.5, 0.0625, ((1, 8),))
    w_key = normal_values(arg_keys[2], (D, KVH * HD), D ** -0.5, 0.0625, ((1, 8),))
    w_value = normal_values(arg_keys[3], (D, KVH * HD), D ** -0.5, 0.0625, ((1, 8),))
    w_out = normal_values(arg_keys[4], (QH * HD, D), 3 ** -0.5, 3.5, ((0, 8),))
    pool_keys = draw_pool_keys(jax.random.fold_in(arg_keys[9], 71), 0)
    pool_values = normal_values(arg_keys[6], (POOL, KVH, HD), 1.0, 6.0, ((0, 16), (1, 8)))
    block_lists = distinct(arg_keys[7], SESSIONS, NBLOCKS, NSEL, 2048)
    offsets = with_ends(jax.random.randint(arg_keys[8], (SESSIONS,), 0, 2048), jax.random.fold_in(arg_keys[8], 1), 0, 2047).astype(jnp.int32)
    return dict(tokens=tokens, w_query=w_query, w_key=w_key, w_value=w_value, w_out=w_out, pool_keys=pool_keys, pool_values=pool_values, block_lists=block_lists, offsets=offsets)


ROPE_BASE = 1000000.0
NEGATIVE = -1e+30

def rotary(values, positions):
    half = values.shape[-1] // 2
    freqs = jnp.exp(jnp.arange(half, dtype=jnp.float32) * (-2.0 * math.log(ROPE_BASE) / values.shape[-1]))
    angles = positions[..., None] * freqs
    cosine = jnp.cos(angles)[..., None, :]
    sine = jnp.sin(angles)[..., None, :]
    first = values[..., :half]
    second = values[..., half:]
    return jnp.concatenate([first * cosine - second * sine, second * cosine + first * sine], axis=-1)

def reference(tokens, w_query, w_key, w_value, w_out, pool_keys, pool_values, block_lists, offsets):
    group = QH // KVH
    scale = 1.0 / math.sqrt(HD)
    query = jnp.dot(tokens, w_query, preferred_element_type=jnp.float32).reshape(SESSIONS, TURN, QH, HD)
    key_new = jnp.dot(tokens, w_key, preferred_element_type=jnp.float32).reshape(SESSIONS, TURN, KVH, HD)
    value_new = jnp.dot(tokens, w_value, preferred_element_type=jnp.float32).astype(jnp.bfloat16).reshape(SESSIONS, TURN, KVH, HD)
    positions = offsets.astype(jnp.float32)[:, None] + jnp.arange(TURN, dtype=jnp.float32)[None, :]
    query = rotary(query, positions).astype(jnp.bfloat16)
    key_new = rotary(key_new, positions).astype(jnp.bfloat16)
    causal = jnp.arange(TURN)[:, None] >= jnp.arange(TURN)[None, :]
    visible = jnp.concatenate([jnp.ones((TURN, NSEL * BLOCK), dtype=bool), causal], axis=1)

    def one_session(inputs):
        session_query, own_keys, own_values, blocks = inputs
        index = (blocks[:, None] * BLOCK + jnp.arange(BLOCK, dtype=jnp.int32)[None, :]).reshape(-1).astype(jnp.int32)
        keys = jnp.concatenate([jnp.take(pool_keys, index, axis=0), own_keys], axis=0).astype(jnp.float32)
        values = jnp.concatenate([jnp.take(pool_values, index, axis=0), own_values], axis=0).astype(jnp.float32)
        grouped = session_query.reshape(TURN, KVH, group, HD).astype(jnp.float32)
        scores = jnp.einsum('ckgd,nkd->kgcn', grouped, keys) * scale
        scores = jnp.where(visible[None, None], scores, NEGATIVE)
        peak = lax.optimization_barrier(jnp.max(scores, axis=-1, keepdims=True))
        weights = jnp.where(visible[None, None], jnp.exp(scores - peak), 0.0)
        total = lax.optimization_barrier(jnp.sum(weights, axis=-1))
        rounded = lax.optimization_barrier(weights.astype(jnp.bfloat16)).astype(jnp.float32)
        mixed = jnp.einsum('kgcn,nkd->kgcd', rounded, values) / total[..., None]
        return jnp.transpose(mixed, (2, 0, 1, 3)).reshape(TURN, QH * HD)
    mixed = lax.map(one_session, (query, key_new, value_new, block_lists))
    mixed = mixed.astype(jnp.bfloat16).reshape(TOKENS, QH * HD)
    return jnp.dot(mixed, w_out, preferred_element_type=jnp.float32).astype(jnp.bfloat16)
```

```python
import functools
import math

import jax
import jax.numpy as jnp
from jax import lax
from jax.experimental import pallas as pl
from jax.experimental.pallas import tpu as pltpu
from jax.sharding import PartitionSpec as P

HD = 128
BLOCK = 512
ROPE_BASE = 1000000.0
NEGATIVE = -1e30
SCALE = math.log2(math.e) / math.sqrt(HD)

NX, NY, NC = 4, 2, 2
NL, NZ = 2, 4


def send(value, dx=0, dy=0, dc=0):
    pairs = []
    for x in range(NX):
        for y in range(NY):
            for c in range(NC):
                src = (x * NY + y) * NC + c
                dst = ((x + dx) % NX * NY + (y + dy) % NY) * NC + (c + dc) % NC
                pairs.append((src, dst))
    return lax.ppermute(value, "blk", pairs)


def send_tp(value, dl=0, dz=0):
    pairs = []
    for l in range(NL):
        for z in range(NZ):
            pairs.append((l * NZ + z, (l + dl) % NL * NZ + (z + dz) % NZ))
    return lax.ppermute(value, "tp", pairs)


def after(value, *done):
    return lax.optimization_barrier((value, *done))[0]


VMEM = pl.BlockSpec(memory_space=pltpu.VMEM)
HBM = pl.BlockSpec(memory_space=pl.ANY)
SMEM = pl.BlockSpec(memory_space=pltpu.SMEM)
ROOMY = pltpu.CompilerParams(vmem_limit_bytes=56 * 1024 * 1024)
PARAMS = pltpu.CompilerParams(vmem_limit_bytes=24 * 1024 * 1024)


WIDE, SLIM = 512, 128
PART = 1024


def project_kernel(count, first, last, ids, *rest):
    chunk_refs = rest[:count]
    wq, wk, wv = rest[count : count + 3]
    rest = rest[count + 3 :]
    if not first:
        acc_in, rest = rest[0], rest[1:]
    if last:
        cos_ref, sin_ref, q_ref, k_ref, v_ref, acc, wbuf, xbuf, sems = rest
    else:
        acc, wbuf, xbuf, sems = rest

    def copies(i):
        rows = pl.ds(pl.multiple_of(ids[i] * PART, PART), PART)
        return (
            pltpu.make_async_copy(wq.at[rows], wbuf.at[i, :, 0:512], sems.at[i, 0]),
            pltpu.make_async_copy(wk.at[rows], wbuf.at[i, :, 512:640], sems.at[i, 1]),
            pltpu.make_async_copy(wv.at[rows], wbuf.at[i, :, 640:768], sems.at[i, 2]),
            pltpu.make_async_copy(chunk_refs[i], xbuf.at[i], sems.at[i, 3]),
        )

    for i in range(count):
        for copy in copies(i):
            copy.start()
    for i in range(count):
        for copy in copies(i):
            copy.wait()
        for low in range(0, WIDE + 2 * SLIM, 256):
            cols = pl.ds(low, 256)
            product = jnp.dot(
                xbuf[i], wbuf[i, :, cols], preferred_element_type=jnp.float32
            )
            if i > 0:
                product = product + acc[:, cols]
            elif not first:
                product = product + acc_in[:, cols]
            acc[:, cols] = product
    if last:
        for s in range(2):
            rows = pl.ds(s * 128, 128)
            cosine, sine = cos_ref[rows], sin_ref[rows]

            def rope(low):
                raw = acc[rows, low : low + HD]
                return (raw * cosine + pltpu.roll(raw, HD // 2, 1) * sine).astype(jnp.bfloat16)

            for g in range(4):
                q_ref[s, g * 128 : (g + 1) * 128] = rope(g * HD)
            k_ref[s] = rope(WIDE)
            v_ref[s] = acc[rows, WIDE + SLIM :].astype(jnp.bfloat16)


def project(chunks, ids, weights, acc=None, tables=None):
    count = len(chunks)
    first, last = acc is None, tables is not None
    full = jax.ShapeDtypeStruct((256, WIDE + 2 * SLIM), jnp.float32)
    scratch = [
        pltpu.VMEM((count, PART, WIDE + 2 * SLIM), jnp.bfloat16),
        pltpu.VMEM((count, 256, PART), jnp.bfloat16),
        pltpu.SemaphoreType.DMA((count, 4)),
    ]
    operands = [ids, *chunks, *weights]
    specs = [SMEM] + [HBM] * (count + 3)
    if not first:
        operands.append(acc)
        specs.append(VMEM)
    if last:
        operands += list(tables)
        specs += [VMEM, VMEM]
        out_shape = [
            jax.ShapeDtypeStruct((2, 512, HD), jnp.bfloat16),
            jax.ShapeDtypeStruct((2, 128, HD), jnp.bfloat16),
            jax.ShapeDtypeStruct((2, 128, HD), jnp.bfloat16),
        ]
        out_specs = [VMEM] * 3
        scratch = [pltpu.VMEM(full.shape, jnp.float32)] + scratch
    else:
        out_shape, out_specs = full, VMEM
    return pl.pallas_call(
        functools.partial(project_kernel, count, first, last),
        out_shape=out_shape,
        in_specs=specs,
        out_specs=out_specs,
        scratch_shapes=scratch,
        compiler_params=ROOMY,
        cost_estimate=pl.CostEstimate(
            flops=2 * 256 * PART * 768 * count, bytes_accessed=count * (8 << 20), transcendentals=0
        ),
        name="project",
    )(*operands)


UNITS = [(dx, dc) for dx in range(NX) for dc in range(NC)]


def fold(query, key, value, state, live=None):
    rows = query.shape[0]
    scores = lax.dot_general(
        query, key, (((1,), (1,)), ((), ())), preferred_element_type=jnp.float32
    )
    parts = [scores[:, i : i + HD] for i in range(0, scores.shape[1], HD)]
    if live is not None:
        parts = [jnp.where(live, part, NEGATIVE) for part in parts]
    peak = jnp.max(functools.reduce(jnp.maximum, parts), axis=-1, keepdims=True)
    peak = jnp.broadcast_to(peak, (rows, HD))
    if state is not None:
        peak = jnp.maximum(peak, state[0])
    weights = jnp.concatenate(
        [jnp.exp2((part - peak) * SCALE).astype(jnp.bfloat16) for part in parts], axis=1
    )
    wide = jnp.concatenate([value, jnp.ones_like(value)], axis=1)
    both = jnp.dot(weights, wide, preferred_element_type=jnp.float32)
    mixed, total = both[:, :HD], both[:, HD:]
    if state is not None:
        shrink = jnp.exp2((state[0] - peak) * SCALE)
        total = total + state[1] * shrink
        mixed = mixed + state[2] * shrink
    return peak, total, mixed


def attend_kernel(own, first, sessions, ordered, codes, q_ref, *rest):
    slots = 8 * sessions
    if own:
        ko_ref, vo_ref, rest = rest[0], rest[1], rest[2:]
    units = {}
    rest = list(rest)
    for key in UNITS:
        if key[0] == 2:
            units[key] = (rest.pop(0).at[0], rest.pop(0).at[0])
        else:
            ref = rest.pop(0)
            units[key] = (ref.at[0], ref.at[1])
    if ordered:
        rest.pop(0)
    if own:
        out_ref, lse_ref, kbuf, vbuf, sems, m_ref, l_ref, o_ref = rest[:8]
        qbuf, extra_sems, kobuf, vobuf = rest[8:]
    else:
        out_ref, kbuf, vbuf, sems, m_ref, l_ref, o_ref = rest[:7]
        qbuf, extra_sems, stat_ref = rest[7:]

    def copies(unit, local, slot):
        rows = pl.ds(pl.multiple_of(local * BLOCK, BLOCK), BLOCK)
        return (
            pltpu.make_async_copy(units[unit][0].at[rows], kbuf.at[slot], sems.at[slot, 0]),
            pltpu.make_async_copy(units[unit][1].at[rows], vbuf.at[slot], sems.at[slot, 1]),
        )

    base = first * 8
    late = [pltpu.make_async_copy(q_ref.at[pl.ds(first, sessions)], qbuf, extra_sems.at[0])]
    if own:
        late.append(pltpu.make_async_copy(ko_ref.at[first], kobuf, extra_sems.at[1]))
        late.append(pltpu.make_async_copy(vo_ref.at[first], vobuf, extra_sems.at[2]))
    for copy in late:
        copy.start()

    @pl.loop(0, slots)
    def _(slot):
        code = codes[base + slot]
        local = code & 3

        def fetch(unit):
            for copy in copies(unit, local, slot):
                copy.start()

        def pick(bit, keys):
            if len(keys) == 1:
                fetch(keys[0])
                return
            half = len(keys) // 2

            @pl.when((code & bit) != 0)
            def _():
                pick(bit // 2, keys[half:])

            @pl.when((code & bit) == 0)
            def _():
                pick(bit // 2, keys[:half])

        @pl.when(code >= 0)
        def _():
            pick(16, UNITS)

    for copy in late:
        copy.wait()
    if own:
        live = lax.broadcasted_iota(jnp.int32, (128, 128), 0) >= lax.broadcasted_iota(
            jnp.int32, (128, 128), 1
        )
        for s in range(sessions):
            for g in range(4):
                rows = pl.ds(g * 128, 128)
                m_ref[s, rows], l_ref[s, rows], o_ref[s, rows] = fold(
                    qbuf[s, rows], kobuf[...], vobuf[...], None, live
                )
    else:
        m_ref[...] = jnp.full_like(m_ref, NEGATIVE)
        l_ref[...] = jnp.zeros_like(l_ref)
        o_ref[...] = jnp.zeros_like(o_ref)

    @pl.loop(0, slots)
    def _(slot):
        @pl.when(codes[base + slot] >= 0)
        def _():
            for copy in copies(UNITS[0], 0, slot):
                copy.wait()
            s = slot // 8
            for g in range(4):
                rows = pl.ds(g * 128, 128)
                state = (m_ref[s, rows], l_ref[s, rows], o_ref[s, rows])
                m_ref[s, rows], l_ref[s, rows], o_ref[s, rows] = fold(
                    qbuf[s, rows], kbuf[slot], vbuf[slot], state
                )

    if not own:
        stat_ref[...] = jnp.zeros_like(stat_ref)
    for s in range(sessions):
        for g in range(4):
            rows = pl.ds(g * 128, 128)
            total = l_ref[s, rows]
            if own:
                out_ref[rows] = o_ref[s, rows] / total
                lse_ref[rows] = m_ref[s, rows] * SCALE + jnp.log2(total)
            else:
                some = total > 0
                total = jnp.where(some, total, 1.0)
                at = (s * 4 + g) * 128
                out_ref[at : at + 128] = (o_ref[s, rows] / total).astype(jnp.bfloat16)
                lse = jnp.where(some, m_ref[s, rows] * SCALE + jnp.log2(total), NEGATIVE)
                stat_ref[s * 4 + g : s * 4 + g + 1] = lse.T[0:1]
    if not own:
        left = stat_ref[...]
        for i in range(3):
            part = left.astype(jnp.bfloat16)
            out_ref[1024 + i * 16 : 1040 + i * 16] = part
            left = left - part.astype(jnp.float32)


PACKED = 1024 + 48


def codes_of(lists, blk):
    owner = lists >> 2
    dx = ((owner >> 2) - (blk >> 2)) & 3
    dc = (owner ^ blk) & 1
    near = ((owner ^ blk) & 2) == 0
    return jnp.where(near, dx * 8 + dc * 4 + (lists & 3), -1).astype(jnp.int32)


def attend(codes, query, units, own=None, first=0, after=()):
    flat = []
    for key in UNITS:
        flat += list(units[key]) if key[0] == 2 else [units[key]]
    flat += after
    sessions = 2 if own is None else 1
    wide = pltpu.VMEM((sessions, 512, HD), jnp.float32)
    scratch = [
        pltpu.VMEM((8 * sessions, BLOCK, HD), jnp.bfloat16),
        pltpu.VMEM((8 * sessions, BLOCK, HD), jnp.bfloat16),
        pltpu.SemaphoreType.DMA((8 * sessions, 2)),
        wide,
        wide,
        wide,
        pltpu.VMEM((sessions, 512, HD), jnp.bfloat16),
        pltpu.SemaphoreType.DMA((3,)),
    ]
    extra = [] if own is None else list(own)
    if own is None:
        out_shape = jax.ShapeDtypeStruct((PACKED, HD), jnp.bfloat16)
        out_specs = VMEM
        scratch.append(pltpu.VMEM((16, HD), jnp.float32))
    else:
        out_shape = [jax.ShapeDtypeStruct((512, HD), jnp.float32)] * 2
        out_specs = [VMEM, VMEM]
        scratch += [pltpu.VMEM((128, HD), jnp.bfloat16)] * 2
    return pl.pallas_call(
        functools.partial(attend_kernel, own is not None, first, sessions, len(after) > 0),
        out_shape=out_shape,
        in_specs=[SMEM] + [HBM] * (1 + len(extra) + len(flat)),
        out_specs=out_specs,
        scratch_shapes=scratch,
        compiler_params=PARAMS,
        cost_estimate=pl.CostEstimate(
            flops=sessions << 32, bytes_accessed=sessions << 23, transcendentals=1024 * 2048
        ),
        name="attend_own" if own is not None else "attend_partner",
    )(codes, query, *extra, *flat)


def combine_kernel(ids, o0_ref, lse0_ref, o1_ref, lse1_ref, back_ref, left_ref, right_ref, mix_ref):
    stats = sum(
        back_ref[1024 + i * 16 : 1040 + i * 16].astype(jnp.float32) for i in range(3)
    )
    for s, (o_ref, lse_ref) in enumerate(((o0_ref, lse0_ref), (o1_ref, lse1_ref))):
        for g in range(4):
            rows = pl.ds(g * 128, 128)
            at = s * 4 + g
            mine = lse_ref[rows]
            other = jnp.broadcast_to(stats[at : at + 1], (128, HD)).T
            top = jnp.maximum(mine, other)
            a, b = jnp.exp2(mine - top), jnp.exp2(other - top)
            back = back_ref[at * 128 : at * 128 + 128].astype(jnp.float32)
            mixed = (o_ref[rows] * a + back * b) / (a + b)
            mix_ref[s * 128 : s * 128 + 128, g * 128 : g * 128 + 128] = mixed.astype(jnp.bfloat16)
    for dl in range(NL):
        for dz in range(NZ):
            piece = mix_ref[pl.ds(pl.multiple_of(ids[dl * NZ + dz] * 32, 32), 32)]
            left_ref[(dl * NZ + dz) * 32 : (dl * NZ + dz + 1) * 32] = piece
            at = (dz + NZ - 1) % NZ * NL + dl
            right_ref[at * 32 : (at + 1) * 32] = piece


def combine(ids, own0, own1, back):
    return pl.pallas_call(
        combine_kernel,
        out_shape=[jax.ShapeDtypeStruct((256, 512), jnp.bfloat16)] * 2,
        in_specs=[SMEM] + [VMEM] * 5,
        out_specs=[VMEM, VMEM],
        scratch_shapes=[pltpu.VMEM((256, 512), jnp.bfloat16)],
        compiler_params=PARAMS,
        cost_estimate=pl.CostEstimate(flops=1 << 20, bytes_accessed=2 << 20, transcendentals=1 << 18),
        name="combine",
    )(ids, *own0, *own1, back)


TILE = 1024


def output_kernel(mix_ref, w_ref, *out_refs):
    for low in range(0, TILE, 256):
        cols = pl.ds(low, 256)
        product = jnp.dot(mix_ref[...], w_ref[:, cols], preferred_element_type=jnp.float32)
        at = 0
        for ref in out_refs:
            ref[:, cols] = product[at : at + ref.shape[0]].astype(jnp.bfloat16)
            at += ref.shape[0]


def output(mix, w_out, start, columns, block, splits):
    tile0 = start // TILE
    rows = sum(splits)
    return pl.pallas_call(
        output_kernel,
        grid=(columns // TILE,),
        out_shape=[jax.ShapeDtypeStruct((n, columns), jnp.bfloat16) for n in splits],
        in_specs=[
            pl.BlockSpec((rows, 512), lambda i: (block, 0)),
            pl.BlockSpec((512, TILE), lambda i: (0, i + tile0)),
        ],
        out_specs=[pl.BlockSpec((n, TILE), lambda i: (0, i)) for n in splits],
        compiler_params=PARAMS,
        cost_estimate=pl.CostEstimate(
            flops=2 * 256 * 512 * columns, bytes_accessed=1024 * columns, transcendentals=0
        ),
        name="output",
    )(mix, w_out)


def add(*terms):
    return sum(term.astype(jnp.float32) for term in terms).astype(jnp.bfloat16)


def project_out(ids, left, right, w_out):
    width = w_out.shape[1]
    half = width // 2
    (there,) = output(left, w_out, 0, half, 1, (128,))
    right = after(right, there)
    there = send_tp(there, dl=1)
    r1, r2, r3 = output(right, w_out, half, half, 0, (64, 64, 64))
    r1 = send_tp(r1, dz=1)
    r3 = send_tp(r3, dz=-1)
    r2 = send_tp(r2, dz=2)
    (here,) = output(left, w_out, 0, half, 0, (128,))
    (r0,) = output(right, w_out, half, half, 3, (64,))
    along = [r0, r1, r3, r2]
    back = send_tp(add(*[v[32:] for v in along]), dl=1)
    first = [(here[i * 32 : i * 32 + 32], there[i * 32 : i * 32 + 32]) for i in range(NZ)]
    l1 = send_tp(add(*first[1]), dz=1)
    l3 = send_tp(add(*first[3]), dz=-1)
    l2 = send_tp(add(*first[2]), dz=2)
    return jnp.concatenate(
        [add(*first[0], l1, l3, l2), add(*[v[:32] for v in along], back)], axis=1
    )


def rope_tables(offsets):
    half = HD // 2
    positions = offsets.astype(jnp.float32)[:, None] + jnp.arange(128, dtype=jnp.float32)[None, :]
    freqs = jnp.exp(jnp.arange(half, dtype=jnp.float32) * (-2.0 * math.log(ROPE_BASE) / HD))
    angles = positions.reshape(-1)[:, None] * freqs
    cosine, sine = jnp.cos(angles), jnp.sin(angles)
    return (
        jnp.concatenate([cosine, cosine], axis=1),
        jnp.concatenate([-sine, sine], axis=1),
    )


def per_device(
    tokens, w_query, w_key, w_value, w_out, pool_keys, pool_values, block_lists, offsets
):
    blk = lax.axis_index("blk")
    tp = lax.axis_index("tp")
    lo, z = tp // NZ, tp % NZ

    def peer(dl, dz):
        return (lo + dl) % NL * NZ + (z + dz) % NZ

    lists = block_lists.reshape(-1)
    codes = codes_of(lists, blk)
    weights = (w_query, w_key, w_value)
    tables = rope_tables(offsets)

    own = jnp.stack([pool_keys[:, 0], pool_values[:, 0]])
    t_y = send_tp(tokens, dl=1)
    t_o = send_tp(tokens, dz=2)
    t_m = send_tp(tokens, dz=1)
    units = {(0, 0): own, (3, 0): send(own, dx=1), (1, 0): send(own, dx=-1)}
    acc = project([tokens, t_y], jnp.stack([tp, peer(1, 0)]), weights)
    t_yo = send_tp(after(t_o, acc), dl=1)
    t_ym = send_tp(t_y, dz=1)
    t_yp = send_tp(t_y, dz=-1)
    t_p = send_tp(after(tokens, t_y), dz=-1)
    units[2, 0] = (send(units[3, 0][:1], dx=1), send(units[1, 0][1:], dx=-1))
    acc = project([t_m, t_o], jnp.stack([peer(0, -1), peer(0, 2)]), weights, acc)
    late = after(own, acc)
    units[0, 1] = send(late, dc=1)
    partner_codes = codes_of(send(after(lists, t_y), dy=1), blk)
    for dx in (1, 3):
        units[dx, 1] = send(units[dx, 0], dc=1)
    units[2, 1] = tuple(send(array, dc=1) for array in units[2, 0])

    acc = project([t_p, t_ym], jnp.stack([peer(0, 1), peer(1, -1)]), weights, acc)
    query, key_new, value_new = project(
        [t_yp, t_yo], jnp.stack([peer(1, 1), peer(1, 2)]), weights, acc, tables
    )

    partner_query = send(query, dy=1)
    own0 = attend(codes, query, units, (key_new, value_new), 0)
    packed = attend(partner_codes, partner_query, units, after=[own0[1]])
    back = send(packed, dy=1)
    own1 = attend(codes, query, units, (key_new, value_new), 1)
    ids = jnp.stack([peer(dl, dz) for dl in range(NL) for dz in range(NZ)])
    left, right = combine(ids, own0, own1, back)
    return project_out(ids, left, right, w_out)


def solution(mesh):
    in_specs = (
        P("blk", "tp"),
        P(None, "tp"),
        P(None, "tp"),
        P(None, "tp"),
        P("tp", None),
        P("blk", "tp", None),
        P("blk", "tp", None),
        P("blk", None),
        P("blk"),
    )
    out_specs = P(("blk", "tp"), None)
    return jax.shard_map(
        per_device, mesh=mesh, in_specs=in_specs, out_specs=out_specs, check_vma=False
    )
```

```python
import functools
import math

import jax
import jax.numpy as jnp
from jax import lax
from jax.experimental import pallas as pl
from jax.experimental.pallas import tpu as pltpu
from jax.sharding import PartitionSpec as P

HD = 128
BLOCK = 512
ROPE_BASE = 1000000.0
NEGATIVE = -1e30
SCALE = math.log2(math.e) / math.sqrt(HD)

NX, NY, NC = 4, 2, 2
NL, NZ = 2, 4


def send(value, dx=0, dy=0, dc=0):
    pairs = []
    for x in range(NX):
        for y in range(NY):
            for c in range(NC):
                src = (x * NY + y) * NC + c
                dst = ((x + dx) % NX * NY + (y + dy) % NY) * NC + (c + dc) % NC
                pairs.append((src, dst))
    return lax.ppermute(value, "blk", pairs)


def send_tp(value, dl=0, dz=0):
    pairs = []
    for l in range(NL):
        for z in range(NZ):
            pairs.append((l * NZ + z, (l + dl) % NL * NZ + (z + dz) % NZ))
    return lax.ppermute(value, "tp", pairs)


def after(value, *done):
    return lax.optimization_barrier((value, *done))[0]


SMALL = pl.CostEstimate(flops=1 << 16, bytes_accessed=1 << 14, transcendentals=0)
LONG = pl.CostEstimate(flops=8 << 30, bytes_accessed=16 << 20, transcendentals=0)
VMEM = pl.BlockSpec(memory_space=pltpu.VMEM)
HBM = pl.BlockSpec(memory_space=pl.ANY)
SMEM = pl.BlockSpec(memory_space=pltpu.SMEM)
def roomy(mebibytes):
    return pltpu.CompilerParams(vmem_limit_bytes=mebibytes * 1024 * 1024)


PARAMS = pltpu.CompilerParams(vmem_limit_bytes=24 * 1024 * 1024)


WIDE, SLIM = 512, 128
PART = 1024


def weight_copies(ids, weights, out, sems, base, i):
    rows = pl.ds(pl.multiple_of(ids[base + i] * PART, PART), PART)
    low = 0
    copies = []
    for j, ref in enumerate(weights):
        width = ref.shape[1]
        copies.append(
            pltpu.make_async_copy(ref.at[rows], out.at[i, :, low : low + width], sems.at[base + i, j])
        )
        low += width
    return copies


def accumulate(ids, chunks, weights, acc, acc_in, wbuf, xbuf, sems):
    copies = []
    for i, chunk in enumerate(chunks):
        copies.append(
            weight_copies(ids, weights, wbuf, sems, 0, i)
            + [pltpu.make_async_copy(chunk, xbuf.at[i], sems.at[i, 3])]
        )
        for copy in copies[i]:
            copy.start()
    for i in range(len(chunks)):
        for copy in copies[i]:
            copy.wait()
        for low in range(0, WIDE + 2 * SLIM, 256):
            cols = pl.ds(low, 256)
            product = jnp.dot(xbuf[i], wbuf[i, :, cols], preferred_element_type=jnp.float32)
            before = acc_in if i == 0 else acc
            acc[:, cols] = product if before is None else product + before[:, cols]


BUFS = [
    pltpu.VMEM((4, PART, WIDE + 2 * SLIM), jnp.bfloat16),
    pltpu.VMEM((4, 256, PART), jnp.bfloat16),
    pltpu.SemaphoreType.DMA((4, 4)),
]


def first_kernel(ids, t0, t1, t2, t3, wq, wk, wv, acc, wbuf, xbuf, sems):
    accumulate(ids, (t0, t1, t2, t3), (wq, wk, wv), acc, None, wbuf, xbuf, sems)


def project_first(ids, chunks, weights):
    return pl.pallas_call(
        first_kernel,
        out_shape=jax.ShapeDtypeStruct((256, WIDE + 2 * SLIM), jnp.float32),
        in_specs=[SMEM] + [HBM] * 7,
        out_specs=VMEM,
        scratch_shapes=BUFS,
        compiler_params=roomy(60),
        cost_estimate=SMALL,
        name="project_first",
    )(ids, *chunks, *weights)


def last_kernel(ids, z_ref, y0_ref, y1_ref, wq, wk, wv, *rest):
    acc_in, cos_ref, sin_ref, q_ref, kv_ref, acc, wbuf, xbuf, sems = rest
    chunks = (z_ref.at[0:256], z_ref.at[256:512], y0_ref, y1_ref)
    accumulate(ids, chunks, (wq, wk, wv), acc, acc_in, wbuf, xbuf, sems)
    for s in range(2):
        rows = pl.ds(s * 128, 128)
        cosine, sine = cos_ref[rows], sin_ref[rows]

        def rope(low):
            raw = acc[rows, low : low + HD]
            return (raw * cosine + pltpu.roll(raw, HD // 2, 1) * sine).astype(jnp.bfloat16)

        for g in range(4):
            q_ref[s, g * 128 : (g + 1) * 128] = rope(g * HD)
        kv_ref[s] = rope(WIDE)
        kv_ref[2 + s] = acc[rows, WIDE + SLIM :].astype(jnp.bfloat16)


def project_last(ids, chunks, weights, acc, tables):
    return pl.pallas_call(
        last_kernel,
        out_shape=[
            jax.ShapeDtypeStruct((2, 512, HD), jnp.bfloat16),
            jax.ShapeDtypeStruct((4, 128, HD), jnp.bfloat16),
        ],
        in_specs=[SMEM] + [HBM] * 6 + [VMEM] * 3,
        out_specs=[VMEM] * 2,
        scratch_shapes=[pltpu.VMEM((256, WIDE + 2 * SLIM), jnp.float32)] + BUFS,
        compiler_params=roomy(60),
        cost_estimate=SMALL,
        name="project_last",
    )(ids, *chunks, *weights, acc, *tables)


UNITS = [(dx, dc) for dx in range(NX) for dc in range(NC)]


def fold(query, key, value, state, live=None):
    rows = query.shape[0]
    scores = lax.dot_general(
        query, key, (((1,), (1,)), ((), ())), preferred_element_type=jnp.float32
    )
    parts = [scores[:, i : i + HD] for i in range(0, scores.shape[1], HD)]
    if live is not None:
        parts = [jnp.where(live, part, NEGATIVE) for part in parts]
    peak = jnp.max(functools.reduce(jnp.maximum, parts), axis=-1, keepdims=True)
    peak = jnp.broadcast_to(peak, (rows, HD))
    if state is not None:
        peak = jnp.maximum(peak, state[0])
    weights = jnp.concatenate(
        [jnp.exp2((part - peak) * SCALE).astype(jnp.bfloat16) for part in parts], axis=1
    )
    wide = jnp.concatenate([value, jnp.ones_like(value)], axis=1)
    both = jnp.dot(weights, wide, preferred_element_type=jnp.float32)
    mixed, total = both[:, :HD], both[:, HD:]
    if state is not None:
        shrink = jnp.exp2((state[0] - peak) * SCALE)
        total = total + state[1] * shrink
        mixed = mixed + state[2] * shrink
    return peak, total, mixed


def attend_kernel(own, first, sessions, ordered, codes, q_ref, *rest):
    slots = 8 * sessions
    if own:
        kv_ref, rest = rest[0], rest[1:]
    units = {}
    rest = list(rest)
    for key in UNITS:
        if key[0] == 2:
            units[key] = (rest.pop(0).at[0], rest.pop(0).at[0])
        else:
            ref = rest.pop(0)
            units[key] = (ref.at[0], ref.at[1])
    if ordered:
        rest.pop(0)
    if own:
        out_ref, lse_ref, kbuf, vbuf, sems, m_ref, l_ref, o_ref = rest[:8]
        qbuf, extra_sems, kobuf, vobuf = rest[8:]
    else:
        out_ref, kbuf, vbuf, sems, m_ref, l_ref, o_ref = rest[:7]
        qbuf, extra_sems, stat_ref = rest[7:]

    def copies(unit, local, slot):
        rows = pl.ds(pl.multiple_of(local * BLOCK, BLOCK), BLOCK)
        return (
            pltpu.make_async_copy(units[unit][0].at[rows], kbuf.at[slot], sems.at[slot, 0]),
            pltpu.make_async_copy(units[unit][1].at[rows], vbuf.at[slot], sems.at[slot, 1]),
        )

    base = first * 8
    late = [pltpu.make_async_copy(q_ref.at[pl.ds(first, sessions)], qbuf, extra_sems.at[0])]
    if own:
        late.append(pltpu.make_async_copy(kv_ref.at[first], kobuf, extra_sems.at[1]))
        late.append(pltpu.make_async_copy(kv_ref.at[2 + first], vobuf, extra_sems.at[2]))
    for copy in late:
        copy.start()

    @pl.loop(0, slots)
    def _(slot):
        code = codes[base + slot]
        local = code & 3

        def fetch(unit):
            for copy in copies(unit, local, slot):
                copy.start()

        def pick(bit, keys):
            if len(keys) == 1:
                fetch(keys[0])
                return
            half = len(keys) // 2

            @pl.when((code & bit) != 0)
            def _():
                pick(bit // 2, keys[half:])

            @pl.when((code & bit) == 0)
            def _():
                pick(bit // 2, keys[:half])

        @pl.when(code >= 0)
        def _():
            pick(16, UNITS)

    for copy in late:
        copy.wait()
    if own:
        live = lax.broadcasted_iota(jnp.int32, (128, 128), 0) >= lax.broadcasted_iota(
            jnp.int32, (128, 128), 1
        )
        for s in range(sessions):
            for g in range(4):
                rows = pl.ds(g * 128, 128)
                m_ref[s, rows], l_ref[s, rows], o_ref[s, rows] = fold(
                    qbuf[s, rows], kobuf[...], vobuf[...], None, live
                )
    else:
        m_ref[...] = jnp.full_like(m_ref, NEGATIVE)
        l_ref[...] = jnp.zeros_like(l_ref)
        o_ref[...] = jnp.zeros_like(o_ref)

    @pl.loop(0, slots)
    def _(slot):
        @pl.when(codes[base + slot] >= 0)
        def _():
            for copy in copies(UNITS[0], 0, slot):
                copy.wait()
            s = slot // 8
            for g in range(4):
                rows = pl.ds(g * 128, 128)
                state = (m_ref[s, rows], l_ref[s, rows], o_ref[s, rows])
                m_ref[s, rows], l_ref[s, rows], o_ref[s, rows] = fold(
                    qbuf[s, rows], kbuf[slot], vbuf[slot], state
                )

    if not own:
        stat_ref[...] = jnp.zeros_like(stat_ref)
    for s in range(sessions):
        for g in range(4):
            rows = pl.ds(g * 128, 128)
            total = l_ref[s, rows]
            if own:
                out_ref[rows] = o_ref[s, rows] / total
                lse_ref[rows] = m_ref[s, rows] * SCALE + jnp.log2(total)
            else:
                some = total > 0
                total = jnp.where(some, total, 1.0)
                at = (s * 4 + g) * 128
                out_ref[at : at + 128] = (o_ref[s, rows] / total).astype(jnp.bfloat16)
                lse = jnp.where(some, m_ref[s, rows] * SCALE + jnp.log2(total), NEGATIVE)
                stat_ref[s * 4 + g : s * 4 + g + 1] = lse.T[0:1]
    if not own:
        left = stat_ref[...]
        for i in range(3):
            part = left.astype(jnp.bfloat16)
            out_ref[1024 + i * 16 : 1040 + i * 16] = part
            left = left - part.astype(jnp.float32)


PACKED = 1024 + 48


def codes_of(lists, blk):
    owner = lists >> 2
    dx = ((owner >> 2) - (blk >> 2)) & 3
    dc = (owner ^ blk) & 1
    near = ((owner ^ blk) & 2) == 0
    return jnp.where(near, dx * 8 + dc * 4 + (lists & 3), -1).astype(jnp.int32)


def attend(codes, query, units, own=None, first=0, after=()):
    flat = []
    for key in UNITS:
        flat += list(units[key]) if key[0] == 2 else [units[key]]
    flat += after
    sessions = 2 if own is None else 1
    wide = pltpu.VMEM((sessions, 512, HD), jnp.float32)
    scratch = [
        pltpu.VMEM((8 * sessions, BLOCK, HD), jnp.bfloat16),
        pltpu.VMEM((8 * sessions, BLOCK, HD), jnp.bfloat16),
        pltpu.SemaphoreType.DMA((8 * sessions, 2)),
        wide,
        wide,
        wide,
        pltpu.VMEM((sessions, 512, HD), jnp.bfloat16),
        pltpu.SemaphoreType.DMA((3,)),
    ]
    extra = [] if own is None else [own]
    if own is None:
        out_shape = jax.ShapeDtypeStruct((PACKED, HD), jnp.bfloat16)
        out_specs = VMEM
        scratch.append(pltpu.VMEM((16, HD), jnp.float32))
    else:
        out_shape = [jax.ShapeDtypeStruct((512, HD), jnp.float32)] * 2
        out_specs = [VMEM, VMEM]
        scratch += [pltpu.VMEM((128, HD), jnp.bfloat16)] * 2
    return pl.pallas_call(
        functools.partial(attend_kernel, own is not None, first, sessions, len(after) > 0),
        out_shape=out_shape,
        in_specs=[SMEM] + [HBM] * (1 + len(extra) + len(flat)),
        out_specs=out_specs,
        scratch_shapes=scratch,
        compiler_params=PARAMS,
        cost_estimate=SMALL if own is not None and first == 0 else LONG,
        name="attend_own" if own is not None else "attend_partner",
    )(codes, query, *extra, *flat)


def combine_kernel(ids, o0_ref, lse0_ref, o1_ref, lse1_ref, back_ref, left_ref, right_ref, mix_ref):
    stats = sum(
        back_ref[1024 + i * 16 : 1040 + i * 16].astype(jnp.float32) for i in range(3)
    )
    for s, (o_ref, lse_ref) in enumerate(((o0_ref, lse0_ref), (o1_ref, lse1_ref))):
        for g in range(4):
            rows = pl.ds(g * 128, 128)
            at = s * 4 + g
            mine = lse_ref[rows]
            other = jnp.broadcast_to(stats[at : at + 1], (128, HD)).T
            top = jnp.maximum(mine, other)
            a, b = jnp.exp2(mine - top), jnp.exp2(other - top)
            back = back_ref[at * 128 : at * 128 + 128].astype(jnp.float32)
            mixed = (o_ref[rows] * a + back * b) / (a + b)
            mix_ref[s * 128 : s * 128 + 128, g * 128 : g * 128 + 128] = mixed.astype(jnp.bfloat16)
    for dl in range(NL):
        for dz in range(NZ):
            piece = mix_ref[pl.ds(pl.multiple_of(ids[dl * NZ + dz] * 32, 32), 32)]
            left_ref[(dl * NZ + dz) * 32 : (dl * NZ + dz + 1) * 32] = piece
            at = (dz + NZ - 1) % NZ * NL + dl
            right_ref[at * 32 : (at + 1) * 32] = piece


def combine(ids, own0, own1, back):
    return pl.pallas_call(
        combine_kernel,
        out_shape=[jax.ShapeDtypeStruct((256, 512), jnp.bfloat16)] * 2,
        in_specs=[SMEM] + [VMEM] * 5,
        out_specs=[VMEM, VMEM],
        scratch_shapes=[pltpu.VMEM((256, 512), jnp.bfloat16)],
        compiler_params=PARAMS,
        cost_estimate=pl.CostEstimate(flops=1 << 20, bytes_accessed=2 << 20, transcendentals=1 << 18),
        name="combine",
    )(ids, *own0, *own1, back)


def output_kernel(mix_ref, w_ref, *out_refs):
    for low in range(0, w_ref.shape[1], 256):
        cols = pl.ds(low, 256)
        product = jnp.dot(mix_ref[...], w_ref[:, cols], preferred_element_type=jnp.float32)
        at = 0
        for ref in out_refs:
            ref[:, cols] = product[at : at + ref.shape[0]].astype(jnp.bfloat16)
            at += ref.shape[0]


def output(mix, w_out, start, columns, tile, block, splits):
    tile0 = start // tile
    rows = sum(splits)
    return pl.pallas_call(
        output_kernel,
        grid=(columns // tile,),
        out_shape=[jax.ShapeDtypeStruct((n, columns), jnp.bfloat16) for n in splits],
        in_specs=[
            pl.BlockSpec((rows, 512), lambda i: (block, 0)),
            pl.BlockSpec((512, tile), lambda i: (0, i + tile0)),
        ],
        out_specs=[pl.BlockSpec((n, tile), lambda i: (0, i)) for n in splits],
        compiler_params=PARAMS,
        cost_estimate=pl.CostEstimate(
            flops=2 * 256 * 512 * columns, bytes_accessed=1024 * columns, transcendentals=0
        ),
        name="output",
    )(mix, w_out)


def add(*terms):
    return sum(term.astype(jnp.float32) for term in terms).astype(jnp.bfloat16)


def project_out(ids, left, right, w_out):
    width = w_out.shape[1]
    left_width = width * 7 // 16
    right_width = width - left_width
    (there,) = output(left, w_out, right_width, left_width, 512, 1, (128,))
    right = after(right, there)
    r1, r2, r3 = output(right, w_out, 0, right_width, 1536, 0, (64, 64, 64))
    r1 = send_tp(r1, dz=1)
    r3 = send_tp(r3, dz=-1)
    r2 = send_tp(r2, dz=2)
    there = send_tp(there, dl=1)
    (here,) = output(left, w_out, right_width, left_width, 512, 0, (128,))
    (r0,) = output(right, w_out, 0, right_width, 1536, 3, (64,))
    along = [r0, r1, r3, r2]
    back = send_tp(add(*[v[32:] for v in along]), dl=1)
    first = [(here[i * 32 : i * 32 + 32], there[i * 32 : i * 32 + 32]) for i in range(NZ)]
    l1 = send_tp(add(*first[1]), dz=1)
    l3 = send_tp(add(*first[3]), dz=-1)
    l2 = send_tp(add(*first[2]), dz=2)
    return jnp.concatenate(
        [add(*[v[:32] for v in along], back), add(*first[0], l1, l3, l2)], axis=1
    )


def rope_tables(offsets):
    half = HD // 2
    positions = offsets.astype(jnp.float32)[:, None] + jnp.arange(128, dtype=jnp.float32)[None, :]
    freqs = jnp.exp(jnp.arange(half, dtype=jnp.float32) * (-2.0 * math.log(ROPE_BASE) / HD))
    angles = positions.reshape(-1)[:, None] * freqs
    cosine, sine = jnp.cos(angles), jnp.sin(angles)
    return (
        jnp.concatenate([cosine, cosine], axis=1),
        jnp.concatenate([-sine, sine], axis=1),
    )


def per_device(
    tokens, w_query, w_key, w_value, w_out, pool_keys, pool_values, block_lists, offsets
):
    blk = lax.axis_index("blk")
    tp = lax.axis_index("tp")
    lo, z = tp // NZ, tp % NZ

    def peer(dl, dz):
        return (lo + dl) % NL * NZ + (z + dz) % NZ

    lists = block_lists.reshape(-1)
    codes = codes_of(lists, blk)
    tables = rope_tables(offsets)

    weights = (w_query, w_key, w_value)
    own = jnp.stack([pool_keys[:, 0], pool_values[:, 0]])
    t_y = send_tp(tokens, dl=1)
    t_m = send_tp(tokens, dz=1)
    t_p = send_tp(tokens, dz=-1)
    units = {(0, 0): own, (3, 0): send(own, dx=1), (1, 0): send(own, dx=-1)}
    t_y, t_m, t_p = lax.optimization_barrier((t_y, t_m, t_p))
    z_in = jnp.concatenate([tokens, t_y])
    z_two = send_tp(z_in, dz=2)
    y_m = send_tp(t_m, dl=1)
    ids = jnp.stack([peer(0, 0), peer(1, 0), peer(0, -1), peer(0, 1)])
    acc = project_first(after(ids, z_in), [tokens, t_y, t_m, t_p], weights)
    partner_lists = send(after(lists, z_in), dy=1)
    t_p, acc, partner_lists = lax.optimization_barrier((t_p, acc, partner_lists))
    partner_codes = codes_of(partner_lists, blk)
    y_p = send_tp(t_p, dl=1)
    units[2, 0] = (
        send(after(units[3, 0], y_m)[:1], dx=1),
        send(after(units[1, 0], y_m)[1:], dx=-1),
    )
    for dx in (0, 1, 3):
        units[dx, 1] = send(after(units[dx, 0], z_two), dc=1)
    query, pairs = project_last(
        jnp.stack([peer(0, 2), peer(1, 2), peer(1, -1), peer(1, 1)]),
        [z_two, y_m, y_p],
        weights,
        acc,
        tables,
    )
    units[2, 1] = tuple(send(after(array, query), dc=1) for array in units[2, 0])

    partner_query = send(query, dy=1)
    own0 = attend(codes, query, units, pairs, 0)
    packed = attend(partner_codes, partner_query, units, after=[own0[1]])
    back = send(packed, dy=1)
    own1 = attend(codes, query, units, pairs, 1)
    ids = jnp.stack([peer(dl, dz) for dl in range(NL) for dz in range(NZ)])
    left, right = combine(ids, own0, own1, back)
    return project_out(ids, left, right, w_out)


def solution(mesh):
    in_specs = (
        P("blk", "tp"),
        P(None, "tp"),
        P(None, "tp"),
        P(None, "tp"),
        P("tp", None),
        P("blk", "tp", None),
        P("blk", "tp", None),
        P("blk", None),
        P("blk"),
    )
    out_specs = P(("blk", "tp"), None)
    return jax.shard_map(
        per_device, mesh=mesh, in_specs=in_specs, out_specs=out_specs, check_vma=False
    )
```

```python
import functools
import math

import jax
import jax.numpy as jnp
from jax import lax
from jax.experimental import pallas as pl
from jax.experimental.pallas import tpu as pltpu
from jax.sharding import PartitionSpec as P

HD = 128
BLOCK = 512
ROPE_BASE = 1000000.0
NEGATIVE = -1e30
SCALE = math.log2(math.e) / math.sqrt(HD)

NX, NY, NC = 4, 2, 2
NL, NZ = 2, 4


def send(value, dx=0, dy=0, dc=0):
    pairs = []
    for x in range(NX):
        for y in range(NY):
            for c in range(NC):
                src = (x * NY + y) * NC + c
                dst = ((x + dx) % NX * NY + (y + dy) % NY) * NC + (c + dc) % NC
                pairs.append((src, dst))
    return lax.ppermute(value, "blk", pairs)


def send_tp(value, dl=0, dz=0):
    pairs = []
    for l in range(NL):
        for z in range(NZ):
            pairs.append((l * NZ + z, (l + dl) % NL * NZ + (z + dz) % NZ))
    return lax.ppermute(value, "tp", pairs)


def after(value, *done):
    return lax.optimization_barrier((value, *done))[0]


SMALL = pl.CostEstimate(flops=1 << 16, bytes_accessed=1 << 14, transcendentals=0)
LONG = pl.CostEstimate(flops=8 << 30, bytes_accessed=16 << 20, transcendentals=0)
VMEM = pl.BlockSpec(memory_space=pltpu.VMEM)
HBM = pl.BlockSpec(memory_space=pl.ANY)
SMEM = pl.BlockSpec(memory_space=pltpu.SMEM)
def roomy(mebibytes):
    return pltpu.CompilerParams(vmem_limit_bytes=mebibytes * 1024 * 1024)


PARAMS = pltpu.CompilerParams(vmem_limit_bytes=24 * 1024 * 1024)


WIDE, SLIM = 512, 128
PART = 1024


def weight_copies(ids, weights, out, sems, base, i):
    rows = pl.ds(pl.multiple_of(ids[base + i] * PART, PART), PART)
    low = 0
    copies = []
    for j, ref in enumerate(weights):
        width = ref.shape[1]
        copies.append(
            pltpu.make_async_copy(ref.at[rows], out.at[i, :, low : low + width], sems.at[base + i, j])
        )
        low += width
    return copies


def accumulate(ids, chunks, weights, acc, acc_in, wbuf, xbuf, sems):
    copies = []
    for i, chunk in enumerate(chunks):
        copies.append(
            weight_copies(ids, weights, wbuf, sems, 0, i)
            + [pltpu.make_async_copy(chunk, xbuf.at[i], sems.at[i, 3])]
        )
        for copy in copies[i]:
            copy.start()
    for i in range(len(chunks)):
        for copy in copies[i]:
            copy.wait()
        for low in range(0, WIDE + 2 * SLIM, 256):
            cols = pl.ds(low, 256)
            product = jnp.dot(xbuf[i], wbuf[i, :, cols], preferred_element_type=jnp.float32)
            before = acc_in if i == 0 else acc
            acc[:, cols] = product if before is None else product + before[:, cols]


BUFS = [
    pltpu.VMEM((4, PART, WIDE + 2 * SLIM), jnp.bfloat16),
    pltpu.VMEM((4, 256, PART), jnp.bfloat16),
    pltpu.SemaphoreType.DMA((4, 4)),
]


def first_kernel(ids, t0, t1, t2, t3, wq, wk, wv, acc, wbuf, xbuf, sems):
    accumulate(ids, (t0, t1, t2, t3), (wq, wk, wv), acc, None, wbuf, xbuf, sems)


def project_first(ids, chunks, weights):
    return pl.pallas_call(
        first_kernel,
        out_shape=jax.ShapeDtypeStruct((256, WIDE + 2 * SLIM), jnp.float32),
        in_specs=[SMEM] + [HBM] * 7,
        out_specs=VMEM,
        scratch_shapes=BUFS,
        compiler_params=roomy(60),
        cost_estimate=SMALL,
        name="project_first",
    )(ids, *chunks, *weights)


def last_kernel(ids, z_ref, y0_ref, y1_ref, wq, wk, wv, *rest):
    acc_in, cos_ref, sin_ref, q_ref, kv_ref, acc, wbuf, xbuf, sems = rest
    chunks = (z_ref.at[0:256], z_ref.at[256:512], y0_ref, y1_ref)
    accumulate(ids, chunks, (wq, wk, wv), acc, acc_in, wbuf, xbuf, sems)
    for s in range(2):
        rows = pl.ds(s * 128, 128)
        cosine, sine = cos_ref[rows], sin_ref[rows]

        def rope(low):
            raw = acc[rows, low : low + HD]
            return (raw * cosine + pltpu.roll(raw, HD // 2, 1) * sine).astype(jnp.bfloat16)

        for g in range(4):
            q_ref[s, g * 128 : (g + 1) * 128] = rope(g * HD)
        kv_ref[s] = rope(WIDE)
        kv_ref[2 + s] = acc[rows, WIDE + SLIM :].astype(jnp.bfloat16)


def project_last(ids, chunks, weights, acc, tables):
    return pl.pallas_call(
        last_kernel,
        out_shape=[
            jax.ShapeDtypeStruct((2, 512, HD), jnp.bfloat16),
            jax.ShapeDtypeStruct((4, 128, HD), jnp.bfloat16),
        ],
        in_specs=[SMEM] + [HBM] * 6 + [VMEM] * 3,
        out_specs=[VMEM] * 2,
        scratch_shapes=[pltpu.VMEM((256, WIDE + 2 * SLIM), jnp.float32)] + BUFS,
        compiler_params=roomy(60),
        cost_estimate=SMALL,
        name="project_last",
    )(ids, *chunks, *weights, acc, *tables)


UNITS = [(dx, dc) for dx in range(NX) for dc in range(NC)]


def fold(query, key, value, state, live=None):
    rows = query.shape[0]
    scores = lax.dot_general(
        query, key, (((1,), (1,)), ((), ())), preferred_element_type=jnp.float32
    )
    parts = [scores[:, i : i + HD] for i in range(0, scores.shape[1], HD)]
    if live is not None:
        parts = [jnp.where(live, part, NEGATIVE) for part in parts]
    peak = jnp.max(functools.reduce(jnp.maximum, parts), axis=-1, keepdims=True)
    peak = jnp.broadcast_to(peak, (rows, HD))
    if state is not None:
        peak = jnp.maximum(peak, state[0])
    weights = jnp.concatenate(
        [jnp.exp2((part - peak) * SCALE).astype(jnp.bfloat16) for part in parts], axis=1
    )
    wide = jnp.concatenate([value, jnp.ones_like(value)], axis=1)
    both = jnp.dot(weights, wide, preferred_element_type=jnp.float32)
    mixed, total = both[:, :HD], both[:, HD:]
    if state is not None:
        shrink = jnp.exp2((state[0] - peak) * SCALE)
        total = total + state[1] * shrink
        mixed = mixed + state[2] * shrink
    return peak, total, mixed


def attend_kernel(own, first, sessions, ordered, codes, q_ref, *rest):
    slots = 8 * sessions
    if own:
        kv_ref, rest = rest[0], rest[1:]
    units = {}
    rest = list(rest)
    for key in UNITS:
        if key[0] == 2:
            units[key] = (rest.pop(0).at[0], rest.pop(0).at[0])
        else:
            ref = rest.pop(0)
            units[key] = (ref.at[0], ref.at[1])
    if ordered:
        rest.pop(0)
    if own:
        out_ref, lse_ref, kbuf, vbuf, sems, m_ref, l_ref, o_ref = rest
    else:
        out_ref, kbuf, vbuf, sems, m_ref, l_ref, o_ref, stat_ref = rest

    def copies(unit, local, slot):
        rows = pl.ds(pl.multiple_of(local * BLOCK, BLOCK), BLOCK)
        return (
            pltpu.make_async_copy(units[unit][0].at[rows], kbuf.at[slot], sems.at[slot, 0]),
            pltpu.make_async_copy(units[unit][1].at[rows], vbuf.at[slot], sems.at[slot, 1]),
        )

    base = first * 8
    @pl.loop(0, slots)
    def _(slot):
        code = codes[base + slot]
        local = code & 3

        def fetch(unit):
            for copy in copies(unit, local, slot):
                copy.start()

        def pick(bit, keys):
            if len(keys) == 1:
                fetch(keys[0])
                return
            half = len(keys) // 2

            @pl.when((code & bit) != 0)
            def _():
                pick(bit // 2, keys[half:])

            @pl.when((code & bit) == 0)
            def _():
                pick(bit // 2, keys[:half])

        @pl.when(code >= 0)
        def _():
            pick(16, UNITS)

    if own:
        live = lax.broadcasted_iota(jnp.int32, (128, 128), 0) >= lax.broadcasted_iota(
            jnp.int32, (128, 128), 1
        )
        for s in range(sessions):
            for g in range(4):
                rows = pl.ds(g * 128, 128)
                m_ref[s, rows], l_ref[s, rows], o_ref[s, rows] = fold(
                    q_ref[first + s, rows], kv_ref[first + s], kv_ref[2 + first + s], None, live
                )
    else:
        m_ref[...] = jnp.full_like(m_ref, NEGATIVE)
        l_ref[...] = jnp.zeros_like(l_ref)
        o_ref[...] = jnp.zeros_like(o_ref)

    @pl.loop(0, slots)
    def _(slot):
        @pl.when(codes[base + slot] >= 0)
        def _():
            for copy in copies(UNITS[0], 0, slot):
                copy.wait()
            s = slot // 8
            for g in range(4):
                rows = pl.ds(g * 128, 128)
                state = (m_ref[s, rows], l_ref[s, rows], o_ref[s, rows])
                m_ref[s, rows], l_ref[s, rows], o_ref[s, rows] = fold(
                    q_ref[first + s, rows], kbuf[slot], vbuf[slot], state
                )

    if not own:
        stat_ref[...] = jnp.zeros_like(stat_ref)
    for s in range(sessions):
        for g in range(4):
            rows = pl.ds(g * 128, 128)
            total = l_ref[s, rows]
            if own:
                out_ref[rows] = o_ref[s, rows] / total
                lse_ref[rows] = m_ref[s, rows] * SCALE + jnp.log2(total)
            else:
                some = total > 0
                total = jnp.where(some, total, 1.0)
                at = (s * 4 + g) * 128
                out_ref[at : at + 128] = (o_ref[s, rows] / total).astype(jnp.bfloat16)
                lse = jnp.where(some, m_ref[s, rows] * SCALE + jnp.log2(total), NEGATIVE)
                stat_ref[s * 4 + g : s * 4 + g + 1] = lse.T[0:1]
    if not own:
        left = stat_ref[...]
        for i in range(3):
            part = left.astype(jnp.bfloat16)
            out_ref[1024 + i * 16 : 1040 + i * 16] = part
            left = left - part.astype(jnp.float32)


PACKED = 1024 + 48


def codes_of(lists, blk):
    owner = lists >> 2
    dx = ((owner >> 2) - (blk >> 2)) & 3
    dc = (owner ^ blk) & 1
    near = ((owner ^ blk) & 2) == 0
    return jnp.where(near, dx * 8 + dc * 4 + (lists & 3), -1).astype(jnp.int32)


def attend(codes, query, units, own=None, first=0, after=()):
    flat = []
    for key in UNITS:
        flat += list(units[key]) if key[0] == 2 else [units[key]]
    flat += after
    sessions = 2 if own is None else 1
    wide = pltpu.VMEM((sessions, 512, HD), jnp.float32)
    scratch = [
        pltpu.VMEM((8 * sessions, BLOCK, HD), jnp.bfloat16),
        pltpu.VMEM((8 * sessions, BLOCK, HD), jnp.bfloat16),
        pltpu.SemaphoreType.DMA((8 * sessions, 2)),
        wide,
        wide,
        wide,
    ]
    extra = [] if own is None else [own]
    if own is None:
        out_shape = jax.ShapeDtypeStruct((PACKED, HD), jnp.bfloat16)
        out_specs = VMEM
        scratch.append(pltpu.VMEM((16, HD), jnp.float32))
    else:
        out_shape = [jax.ShapeDtypeStruct((512, HD), jnp.float32)] * 2
        out_specs = [VMEM, VMEM]
    return pl.pallas_call(
        functools.partial(attend_kernel, own is not None, first, sessions, len(after) > 0),
        out_shape=out_shape,
        in_specs=[SMEM] + [VMEM] * (1 + len(extra)) + [HBM] * len(flat),
        out_specs=out_specs,
        scratch_shapes=scratch,
        compiler_params=PARAMS,
        cost_estimate=SMALL if own is not None and first == 0 else LONG,
        name="attend_own" if own is not None else "attend_partner",
    )(codes, query, *extra, *flat)


def combine_kernel(ids, o0_ref, lse0_ref, o1_ref, lse1_ref, back_ref, left_ref, right_ref, mix_ref):
    stats = sum(
        back_ref[1024 + i * 16 : 1040 + i * 16].astype(jnp.float32) for i in range(3)
    )
    for s, (o_ref, lse_ref) in enumerate(((o0_ref, lse0_ref), (o1_ref, lse1_ref))):
        for g in range(4):
            rows = pl.ds(g * 128, 128)
            at = s * 4 + g
            mine = lse_ref[rows]
            other = jnp.broadcast_to(stats[at : at + 1], (128, HD)).T
            top = jnp.maximum(mine, other)
            a, b = jnp.exp2(mine - top), jnp.exp2(other - top)
            back = back_ref[at * 128 : at * 128 + 128].astype(jnp.float32)
            mixed = (o_ref[rows] * a + back * b) / (a + b)
            mix_ref[s * 128 : s * 128 + 128, g * 128 : g * 128 + 128] = mixed.astype(jnp.bfloat16)
    for dl in range(NL):
        for dz in range(NZ):
            piece = mix_ref[pl.ds(pl.multiple_of(ids[dl * NZ + dz] * 32, 32), 32)]
            left_ref[(dl * NZ + dz) * 32 : (dl * NZ + dz + 1) * 32] = piece
            at = (dz + NZ - 1) % NZ * NL + dl
            right_ref[at * 32 : (at + 1) * 32] = piece


def combine(ids, own0, own1, back):
    return pl.pallas_call(
        combine_kernel,
        out_shape=[jax.ShapeDtypeStruct((256, 512), jnp.bfloat16)] * 2,
        in_specs=[SMEM] + [VMEM] * 5,
        out_specs=[VMEM, VMEM],
        scratch_shapes=[pltpu.VMEM((256, 512), jnp.bfloat16)],
        compiler_params=PARAMS,
        cost_estimate=pl.CostEstimate(flops=1 << 20, bytes_accessed=2 << 20, transcendentals=1 << 18),
        name="combine",
    )(ids, *own0, *own1, back)


def output_kernel(mix_ref, w_ref, *out_refs):
    for low in range(0, w_ref.shape[1], 256):
        cols = pl.ds(low, 256)
        product = jnp.dot(mix_ref[...], w_ref[:, cols], preferred_element_type=jnp.float32)
        at = 0
        for ref in out_refs:
            ref[:, cols] = product[at : at + ref.shape[0]].astype(jnp.bfloat16)
            at += ref.shape[0]


TILE = 1024


def output(mix, w_out, start, columns, block, splits):
    tile0 = start // TILE
    rows = sum(splits)
    return pl.pallas_call(
        output_kernel,
        grid=(columns // TILE,),
        out_shape=[jax.ShapeDtypeStruct((n, columns), jnp.bfloat16) for n in splits],
        in_specs=[
            pl.BlockSpec((rows, 512), lambda i: (block, 0)),
            pl.BlockSpec((512, TILE), lambda i: (0, i + tile0)),
        ],
        out_specs=[pl.BlockSpec((n, TILE), lambda i: (0, i)) for n in splits],
        compiler_params=PARAMS,
        cost_estimate=pl.CostEstimate(
            flops=2 * 256 * 512 * columns, bytes_accessed=1024 * columns, transcendentals=0
        ),
        name="output",
    )(mix, w_out)


def add(*terms):
    return sum(term.astype(jnp.float32) for term in terms).astype(jnp.bfloat16)


def project_out(ids, left, right, w_out):
    half = w_out.shape[1] // 2
    parts = [(half, half // 2), (half * 3 // 2, half // 2)]
    r1, r2, r3 = output(right, w_out, 0, half, 0, (64, 64, 64))
    left = after(left, r1)
    r1 = send_tp(r1, dz=1)
    r3 = send_tp(r3, dz=-1)
    r2 = send_tp(r2, dz=2)
    theres = [output(left, w_out, start, width, 1, (128,))[0] for start, width in parts]
    own_rows = after(left, *theres)
    heres = [output(own_rows, w_out, start, width, 0, (128,))[0] for start, width in parts]
    (r0,) = output(after(right, *theres), w_out, 0, half, 3, (64,))
    theres = [send_tp(there, dl=1) for there in theres]
    r0 = after(r0, theres[0])
    along = [r0, r1, r3, r2]
    back = send_tp(add(*[v[32:] for v in along]), dl=1)
    sums = [add(*[v[:32] for v in along], back)]
    for mine, there in zip(heres, theres):
        pairs = [(mine[i * 32 : i * 32 + 32], there[i * 32 : i * 32 + 32]) for i in range(NZ)]
        l1 = send_tp(add(*pairs[1]), dz=1)
        l3 = send_tp(add(*pairs[3]), dz=-1)
        l2 = send_tp(add(*pairs[2]), dz=2)
        sums.append(add(*pairs[0], l1, l3, l2))
    return jnp.concatenate(sums, axis=1)


def rope_tables(offsets):
    half = HD // 2
    positions = offsets.astype(jnp.float32)[:, None] + jnp.arange(128, dtype=jnp.float32)[None, :]
    freqs = jnp.exp(jnp.arange(half, dtype=jnp.float32) * (-2.0 * math.log(ROPE_BASE) / HD))
    angles = positions.reshape(-1)[:, None] * freqs
    cosine, sine = jnp.cos(angles), jnp.sin(angles)
    return (
        jnp.concatenate([cosine, cosine], axis=1),
        jnp.concatenate([-sine, sine], axis=1),
    )


def per_device(
    tokens, w_query, w_key, w_value, w_out, pool_keys, pool_values, block_lists, offsets
):
    blk = lax.axis_index("blk")
    tp = lax.axis_index("tp")
    lo, z = tp // NZ, tp % NZ

    def peer(dl, dz):
        return (lo + dl) % NL * NZ + (z + dz) % NZ

    lists = block_lists.reshape(-1)
    codes = codes_of(lists, blk)
    tables = rope_tables(offsets)

    weights = (w_query, w_key, w_value)
    own = jnp.stack([pool_keys[:, 0], pool_values[:, 0]])
    t_y = send_tp(tokens, dl=1)
    t_m = send_tp(tokens, dz=1)
    t_p = send_tp(tokens, dz=-1)
    units = {(0, 0): own, (3, 0): send(own, dx=1), (1, 0): send(own, dx=-1)}
    t_y, t_m, t_p = lax.optimization_barrier((t_y, t_m, t_p))
    z_in = jnp.concatenate([tokens, t_y])
    z_two = send_tp(z_in, dz=2)
    y_m = send_tp(t_m, dl=1)
    ids = jnp.stack([peer(0, 0), peer(1, 0), peer(0, -1), peer(0, 1)])
    acc = project_first(after(ids, z_in), [tokens, t_y, t_m, t_p], weights)
    partner_lists = send(after(lists, z_in), dy=1)
    t_p, acc, partner_lists = lax.optimization_barrier((t_p, acc, partner_lists))
    partner_codes = codes_of(partner_lists, blk)
    y_p = send_tp(t_p, dl=1)
    units[2, 0] = (
        send(after(units[3, 0], y_m)[:1], dx=1),
        send(after(units[1, 0], y_m)[1:], dx=-1),
    )
    for dx in (0, 1, 3):
        units[dx, 1] = send(after(units[dx, 0], z_two), dc=1)
    query, pairs = project_last(
        jnp.stack([peer(0, 2), peer(1, 2), peer(1, -1), peer(1, 1)]),
        [z_two, y_m, y_p],
        weights,
        acc,
        tables,
    )
    units[2, 1] = tuple(send(after(array, query), dc=1) for array in units[2, 0])

    partner_query = send(query, dy=1)
    own0 = attend(codes, query, units, pairs, 0)
    packed = attend(partner_codes, partner_query, units, after=[own0[1]])
    back = send(packed, dy=1)
    own1 = attend(codes, query, units, pairs, 1)
    ids = jnp.stack([peer(dl, dz) for dl in range(NL) for dz in range(NZ)])
    left, right = combine(ids, own0, own1, back)
    return project_out(ids, left, right, w_out)


def solution(mesh):
    in_specs = (
        P("blk", "tp"),
        P(None, "tp"),
        P(None, "tp"),
        P(None, "tp"),
        P("tp", None),
        P("blk", "tp", None),
        P("blk", "tp", None),
        P("blk", None),
        P("blk"),
    )
    out_specs = P(("blk", "tp"), None)
    return jax.shard_map(
        per_device, mesh=mesh, in_specs=in_specs, out_specs=out_specs, check_vma=False
    )
```

```python
import functools
import math

import jax
import jax.numpy as jnp
from jax import lax
from jax.experimental import pallas as pl
from jax.experimental.pallas import tpu as pltpu
from jax.sharding import PartitionSpec as P

HD = 128
BLOCK = 512
ROPE_BASE = 1000000.0
NEGATIVE = -1e30
SCALE = math.log2(math.e) / math.sqrt(HD)

NX, NY, NC = 4, 2, 2
NL, NZ = 2, 4


def send(value, dx=0, dy=0, dc=0):
    pairs = []
    for x in range(NX):
        for y in range(NY):
            for c in range(NC):
                src = (x * NY + y) * NC + c
                dst = ((x + dx) % NX * NY + (y + dy) % NY) * NC + (c + dc) % NC
                pairs.append((src, dst))
    return lax.ppermute(value, "blk", pairs)


def send_tp(value, dl=0, dz=0):
    pairs = []
    for l in range(NL):
        for z in range(NZ):
            pairs.append((l * NZ + z, (l + dl) % NL * NZ + (z + dz) % NZ))
    return lax.ppermute(value, "tp", pairs)


def after(value, *done):
    return lax.optimization_barrier((value, *done))[0]


SMALL = pl.CostEstimate(flops=1 << 16, bytes_accessed=1 << 14, transcendentals=0)
LONG = pl.CostEstimate(flops=8 << 30, bytes_accessed=16 << 20, transcendentals=0)
VMEM = pl.BlockSpec(memory_space=pltpu.VMEM)
HBM = pl.BlockSpec(memory_space=pl.ANY)
SMEM = pl.BlockSpec(memory_space=pltpu.SMEM)
def roomy(mebibytes):
    return pltpu.CompilerParams(vmem_limit_bytes=mebibytes * 1024 * 1024)


PARAMS = pltpu.CompilerParams(vmem_limit_bytes=24 * 1024 * 1024)


WIDE, SLIM = 512, 128
PART = 1024


def weight_copies(ids, weights, out, sems, base, i):
    rows = pl.ds(pl.multiple_of(ids[base + i] * PART, PART), PART)
    low = 0
    copies = []
    for j, ref in enumerate(weights):
        width = ref.shape[1]
        copies.append(
            pltpu.make_async_copy(ref.at[rows], out.at[i, :, low : low + width], sems.at[base + i, j])
        )
        low += width
    return copies


def accumulate(ids, chunks, weights, acc, acc_in, wbuf, xbuf, sems):
    copies = []
    for i, chunk in enumerate(chunks):
        copies.append(
            weight_copies(ids, weights, wbuf, sems, 0, i)
            + [pltpu.make_async_copy(chunk, xbuf.at[i], sems.at[i, 3])]
        )
        for copy in copies[i]:
            copy.start()
    for i in range(len(chunks)):
        for copy in copies[i]:
            copy.wait()
        for low in range(0, WIDE + 2 * SLIM, 256):
            cols = pl.ds(low, 256)
            product = jnp.dot(xbuf[i], wbuf[i, :, cols], preferred_element_type=jnp.float32)
            before = acc_in if i == 0 else acc
            acc[:, cols] = product if before is None else product + before[:, cols]


BUFS = [
    pltpu.VMEM((4, PART, WIDE + 2 * SLIM), jnp.bfloat16),
    pltpu.VMEM((4, 256, PART), jnp.bfloat16),
    pltpu.SemaphoreType.DMA((4, 4)),
]


def first_kernel(ids, t0, t1, t2, t3, wq, wk, wv, acc, wbuf, xbuf, sems):
    accumulate(ids, (t0, t1, t2, t3), (wq, wk, wv), acc, None, wbuf, xbuf, sems)


def project_first(ids, chunks, weights):
    return pl.pallas_call(
        first_kernel,
        out_shape=jax.ShapeDtypeStruct((256, WIDE + 2 * SLIM), jnp.float32),
        in_specs=[SMEM] + [HBM] * 7,
        out_specs=VMEM,
        scratch_shapes=BUFS,
        compiler_params=roomy(60),
        cost_estimate=SMALL,
        name="project_first",
    )(ids, *chunks, *weights)


def last_kernel(ids, z_ref, y0_ref, y1_ref, wq, wk, wv, *rest):
    acc_in, cos_ref, sin_ref, q_ref, kv_ref, acc, wbuf, xbuf, sems = rest
    chunks = (z_ref.at[0:256], z_ref.at[256:512], y0_ref, y1_ref)
    accumulate(ids, chunks, (wq, wk, wv), acc, acc_in, wbuf, xbuf, sems)
    for s in range(2):
        rows = pl.ds(s * 128, 128)
        cosine, sine = cos_ref[rows], sin_ref[rows]

        def rope(low):
            raw = acc[rows, low : low + HD]
            return (raw * cosine + pltpu.roll(raw, HD // 2, 1) * sine).astype(jnp.bfloat16)

        for g in range(4):
            q_ref[s, g * 128 : (g + 1) * 128] = rope(g * HD)
        kv_ref[s] = rope(WIDE)
        kv_ref[2 + s] = acc[rows, WIDE + SLIM :].astype(jnp.bfloat16)


def project_last(ids, chunks, weights, acc, tables):
    return pl.pallas_call(
        last_kernel,
        out_shape=[
            jax.ShapeDtypeStruct((2, 512, HD), jnp.bfloat16),
            jax.ShapeDtypeStruct((4, 128, HD), jnp.bfloat16),
        ],
        in_specs=[SMEM] + [HBM] * 6 + [VMEM] * 3,
        out_specs=[VMEM] * 2,
        scratch_shapes=[pltpu.VMEM((256, WIDE + 2 * SLIM), jnp.float32)] + BUFS,
        compiler_params=roomy(60),
        cost_estimate=SMALL,
        name="project_last",
    )(ids, *chunks, *weights, acc, *tables)


UNITS = [(dx, dc) for dx in range(NX) for dc in range(NC)]


def fold(query, key, value, state, live=None):
    rows = query.shape[0]
    scores = lax.dot_general(
        query, key, (((1,), (1,)), ((), ())), preferred_element_type=jnp.float32
    )
    parts = [scores[:, i : i + HD] for i in range(0, scores.shape[1], HD)]
    if live is not None:
        parts = [jnp.where(live, part, NEGATIVE) for part in parts]
    peak = jnp.max(functools.reduce(jnp.maximum, parts), axis=-1, keepdims=True)
    peak = jnp.broadcast_to(peak, (rows, HD))
    if state is not None:
        peak = jnp.maximum(peak, state[0])
    weights = jnp.concatenate(
        [jnp.exp2((part - peak) * SCALE).astype(jnp.bfloat16) for part in parts], axis=1
    )
    wide = jnp.concatenate([value, jnp.ones_like(value)], axis=1)
    both = jnp.dot(weights, wide, preferred_element_type=jnp.float32)
    mixed, total = both[:, :HD], both[:, HD:]
    if state is not None:
        shrink = jnp.exp2((state[0] - peak) * SCALE)
        total = total + state[1] * shrink
        mixed = mixed + state[2] * shrink
    return peak, total, mixed


def attend_kernel(own, first, sessions, ordered, codes, q_ref, *rest):
    slots = 8 * sessions
    if own:
        kv_ref, rest = rest[0], rest[1:]
    units = {}
    rest = list(rest)
    for key in UNITS:
        if key[0] == 2:
            units[key] = (rest.pop(0).at[0], rest.pop(0).at[0])
        else:
            ref = rest.pop(0)
            units[key] = (ref.at[0], ref.at[1])
    if ordered:
        rest.pop(0)
    if own:
        out_ref, lse_ref, kbuf, vbuf, sems, m_ref, l_ref, o_ref = rest
    else:
        out_ref, kbuf, vbuf, sems, m_ref, l_ref, o_ref, stat_ref = rest

    def copies(unit, local, slot):
        rows = pl.ds(pl.multiple_of(local * BLOCK, BLOCK), BLOCK)
        return (
            pltpu.make_async_copy(units[unit][0].at[rows], kbuf.at[slot], sems.at[slot, 0]),
            pltpu.make_async_copy(units[unit][1].at[rows], vbuf.at[slot], sems.at[slot, 1]),
        )

    base = first * 8
    @pl.loop(0, slots)
    def _(slot):
        code = codes[base + slot]
        local = code & 3

        def fetch(unit):
            for copy in copies(unit, local, slot):
                copy.start()

        def pick(bit, keys):
            if len(keys) == 1:
                fetch(keys[0])
                return
            half = len(keys) // 2

            @pl.when((code & bit) != 0)
            def _():
                pick(bit // 2, keys[half:])

            @pl.when((code & bit) == 0)
            def _():
                pick(bit // 2, keys[:half])

        @pl.when(code >= 0)
        def _():
            pick(16, UNITS)

    if own:
        live = lax.broadcasted_iota(jnp.int32, (128, 128), 0) >= lax.broadcasted_iota(
            jnp.int32, (128, 128), 1
        )
        for s in range(sessions):
            for g in range(4):
                rows = pl.ds(g * 128, 128)
                m_ref[s, rows], l_ref[s, rows], o_ref[s, rows] = fold(
                    q_ref[first + s, rows], kv_ref[first + s], kv_ref[2 + first + s], None, live
                )
    else:
        m_ref[...] = jnp.full_like(m_ref, NEGATIVE)
        l_ref[...] = jnp.zeros_like(l_ref)
        o_ref[...] = jnp.zeros_like(o_ref)

    @pl.loop(0, slots)
    def _(slot):
        @pl.when(codes[base + slot] >= 0)
        def _():
            for copy in copies(UNITS[0], 0, slot):
                copy.wait()
            s = slot // 8
            for g in range(4):
                rows = pl.ds(g * 128, 128)
                state = (m_ref[s, rows], l_ref[s, rows], o_ref[s, rows])
                m_ref[s, rows], l_ref[s, rows], o_ref[s, rows] = fold(
                    q_ref[first + s, rows], kbuf[slot], vbuf[slot], state
                )

    if not own:
        stat_ref[...] = jnp.zeros_like(stat_ref)
    for s in range(sessions):
        for g in range(4):
            rows = pl.ds(g * 128, 128)
            total = l_ref[s, rows]
            if own:
                out_ref[rows] = o_ref[s, rows] / total
                lse_ref[rows] = m_ref[s, rows] * SCALE + jnp.log2(total)
            else:
                some = total > 0
                total = jnp.where(some, total, 1.0)
                at = (s * 4 + g) * 128
                out_ref[at : at + 128] = (o_ref[s, rows] / total).astype(jnp.bfloat16)
                lse = jnp.where(some, m_ref[s, rows] * SCALE + jnp.log2(total), NEGATIVE)
                stat_ref[s * 4 + g : s * 4 + g + 1] = lse.T[0:1]
    if not own:
        left = stat_ref[...]
        for i in range(3):
            part = left.astype(jnp.bfloat16)
            out_ref[1024 + i * 16 : 1040 + i * 16] = part
            left = left - part.astype(jnp.float32)


PACKED = 1024 + 48


def codes_of(lists, blk):
    owner = lists >> 2
    dx = ((owner >> 2) - (blk >> 2)) & 3
    dc = (owner ^ blk) & 1
    near = ((owner ^ blk) & 2) == 0
    return jnp.where(near, dx * 8 + dc * 4 + (lists & 3), -1).astype(jnp.int32)


def attend(codes, query, units, own=None, first=0, after=()):
    flat = []
    for key in UNITS:
        flat += list(units[key]) if key[0] == 2 else [units[key]]
    flat += after
    sessions = 2 if own is None else 1
    wide = pltpu.VMEM((sessions, 512, HD), jnp.float32)
    scratch = [
        pltpu.VMEM((8 * sessions, BLOCK, HD), jnp.bfloat16),
        pltpu.VMEM((8 * sessions, BLOCK, HD), jnp.bfloat16),
        pltpu.SemaphoreType.DMA((8 * sessions, 2)),
        wide,
        wide,
        wide,
    ]
    extra = [] if own is None else [own]
    if own is None:
        out_shape = jax.ShapeDtypeStruct((PACKED, HD), jnp.bfloat16)
        out_specs = VMEM
        scratch.append(pltpu.VMEM((16, HD), jnp.float32))
    else:
        out_shape = [jax.ShapeDtypeStruct((512, HD), jnp.float32)] * 2
        out_specs = [VMEM, VMEM]
    return pl.pallas_call(
        functools.partial(attend_kernel, own is not None, first, sessions, len(after) > 0),
        out_shape=out_shape,
        in_specs=[SMEM] + [VMEM] * (1 + len(extra)) + [HBM] * len(flat),
        out_specs=out_specs,
        scratch_shapes=scratch,
        compiler_params=PARAMS,
        cost_estimate=SMALL if own is not None and first == 0 else LONG,
        name="attend_own" if own is not None else "attend_partner",
    )(codes, query, *extra, *flat)


def combine_kernel(ids, o0_ref, lse0_ref, o1_ref, lse1_ref, back_ref, left_ref, right_ref, mix_ref):
    stats = sum(
        back_ref[1024 + i * 16 : 1040 + i * 16].astype(jnp.float32) for i in range(3)
    )
    for s, (o_ref, lse_ref) in enumerate(((o0_ref, lse0_ref), (o1_ref, lse1_ref))):
        for g in range(4):
            rows = pl.ds(g * 128, 128)
            at = s * 4 + g
            mine = lse_ref[rows]
            other = jnp.broadcast_to(stats[at : at + 1], (128, HD)).T
            top = jnp.maximum(mine, other)
            a, b = jnp.exp2(mine - top), jnp.exp2(other - top)
            back = back_ref[at * 128 : at * 128 + 128].astype(jnp.float32)
            mixed = (o_ref[rows] * a + back * b) / (a + b)
            mix_ref[s * 128 : s * 128 + 128, g * 128 : g * 128 + 128] = mixed.astype(jnp.bfloat16)
    for dl in range(NL):
        for dz in range(NZ):
            piece = mix_ref[pl.ds(pl.multiple_of(ids[dl * NZ + dz] * 32, 32), 32)]
            left_ref[(dl * NZ + dz) * 32 : (dl * NZ + dz + 1) * 32] = piece
            at = (dz + NZ - 1) % NZ * NL + dl
            right_ref[at * 32 : (at + 1) * 32] = piece


def combine(ids, own0, own1, back):
    return pl.pallas_call(
        combine_kernel,
        out_shape=[jax.ShapeDtypeStruct((256, 512), jnp.bfloat16)] * 2,
        in_specs=[SMEM] + [VMEM] * 5,
        out_specs=[VMEM, VMEM],
        scratch_shapes=[pltpu.VMEM((256, 512), jnp.bfloat16)],
        compiler_params=PARAMS,
        cost_estimate=pl.CostEstimate(flops=1 << 20, bytes_accessed=2 << 20, transcendentals=1 << 18),
        name="combine",
    )(ids, *own0, *own1, back)


def output_kernel(mix_ref, w_ref, *out_refs):
    for low in range(0, w_ref.shape[1], 256):
        cols = pl.ds(low, 256)
        product = jnp.dot(mix_ref[...], w_ref[:, cols], preferred_element_type=jnp.float32)
        at = 0
        for ref in out_refs:
            ref[:, cols] = product[at : at + ref.shape[0]].astype(jnp.bfloat16)
            at += ref.shape[0]


TILE = 512


def output(mix, w_out, start, columns, block, splits):
    tile0 = start // TILE
    rows = sum(splits)
    return pl.pallas_call(
        output_kernel,
        grid=(columns // TILE,),
        out_shape=[jax.ShapeDtypeStruct((n, columns), jnp.bfloat16) for n in splits],
        in_specs=[
            pl.BlockSpec((rows, 512), lambda i: (block, 0)),
            pl.BlockSpec((512, TILE), lambda i: (0, i + tile0)),
        ],
        out_specs=[pl.BlockSpec((n, TILE), lambda i: (0, i)) for n in splits],
        compiler_params=PARAMS,
        cost_estimate=pl.CostEstimate(
            flops=2 * 256 * 512 * columns, bytes_accessed=1024 * columns, transcendentals=0
        ),
        name="output",
    )(mix, w_out)


def add(*terms):
    return sum(term.astype(jnp.float32) for term in terms).astype(jnp.bfloat16)


def project_out(ids, left, right, w_out):
    unit = w_out.shape[1] // 16
    half = unit * 7
    parts = [(half, unit * 4), (unit * 11, unit * 5)]
    r1, r2, r3 = output(right, w_out, 0, half, 0, (64, 64, 64))
    left = after(left, r1)
    r1 = send_tp(r1, dz=1)
    r3 = send_tp(r3, dz=-1)
    r2 = send_tp(r2, dz=2)
    theres = [output(left, w_out, start, width, 1, (128,))[0] for start, width in parts]
    own_rows = after(left, *theres)
    heres = [output(own_rows, w_out, start, width, 0, (128,))[0] for start, width in parts]
    (r0,) = output(after(right, *theres), w_out, 0, half, 3, (64,))
    theres = [send_tp(there, dl=1) for there in theres]
    r0 = after(r0, theres[0])
    along = [r0, r1, r3, r2]
    back = send_tp(add(*[v[32:] for v in along]), dl=1)
    sums = [add(*[v[:32] for v in along], back)]
    for mine, there in zip(heres, theres):
        pairs = [(mine[i * 32 : i * 32 + 32], there[i * 32 : i * 32 + 32]) for i in range(NZ)]
        l1 = send_tp(add(*pairs[1]), dz=1)
        l3 = send_tp(add(*pairs[3]), dz=-1)
        l2 = send_tp(add(*pairs[2]), dz=2)
        sums.append(add(*pairs[0], l1, l3, l2))
    return jnp.concatenate(sums, axis=1)


def rope_tables(offsets):
    half = HD // 2
    positions = offsets.astype(jnp.float32)[:, None] + jnp.arange(128, dtype=jnp.float32)[None, :]
    freqs = jnp.exp(jnp.arange(half, dtype=jnp.float32) * (-2.0 * math.log(ROPE_BASE) / HD))
    angles = positions.reshape(-1)[:, None] * freqs
    cosine, sine = jnp.cos(angles), jnp.sin(angles)
    return (
        jnp.concatenate([cosine, cosine], axis=1),
        jnp.concatenate([-sine, sine], axis=1),
    )


def per_device(
    tokens, w_query, w_key, w_value, w_out, pool_keys, pool_values, block_lists, offsets
):
    blk = lax.axis_index("blk")
    tp = lax.axis_index("tp")
    lo, z = tp // NZ, tp % NZ

    def peer(dl, dz):
        return (lo + dl) % NL * NZ + (z + dz) % NZ

    lists = block_lists.reshape(-1)
    codes = codes_of(lists, blk)
    tables = rope_tables(offsets)

    weights = (w_query, w_key, w_value)
    own = jnp.stack([pool_keys[:, 0], pool_values[:, 0]])
    t_y = send_tp(tokens, dl=1)
    t_m = send_tp(tokens, dz=1)
    t_p = send_tp(tokens, dz=-1)
    units = {(0, 0): own, (3, 0): send(own, dx=1), (1, 0): send(own, dx=-1)}
    t_y, t_m, t_p = lax.optimization_barrier((t_y, t_m, t_p))
    z_in = jnp.concatenate([tokens, t_y])
    z_two = send_tp(z_in, dz=2)
    y_m = send_tp(t_m, dl=1)
    ids = jnp.stack([peer(0, 0), peer(1, 0), peer(0, -1), peer(0, 1)])
    acc = project_first(after(ids, z_in), [tokens, t_y, t_m, t_p], weights)
    t_p, acc = lax.optimization_barrier((t_p, acc))
    y_p = send_tp(t_p, dl=1)
    far_k, far_v = after(units[3, 0], y_m)[:1], after(units[1, 0], y_m)[1:]
    units[2, 0] = (send(far_k, dx=1), send(far_v, dx=-1))
    acc, partner_lists = lax.optimization_barrier((acc, send(after(lists, far_k, far_v), dy=1)))
    partner_codes = codes_of(partner_lists, blk)
    for dx in (0, 1, 3):
        units[dx, 1] = send(after(units[dx, 0], z_two), dc=1)
    query, pairs = project_last(
        jnp.stack([peer(0, 2), peer(1, 2), peer(1, -1), peer(1, 1)]),
        [z_two, y_m, y_p],
        weights,
        acc,
        tables,
    )
    units[2, 1] = tuple(send(after(array, query), dc=1) for array in units[2, 0])

    partner_query = send(query, dy=1)
    own0 = attend(codes, query, units, pairs, 0)
    packed = attend(partner_codes, partner_query, units, after=[own0[1]])
    back = send(packed, dy=1)
    own1 = attend(codes, query, units, pairs, 1)
    ids = jnp.stack([peer(dl, dz) for dl in range(NL) for dz in range(NZ)])
    left, right = combine(ids, own0, own1, back)
    return project_out(ids, left, right, w_out)


def solution(mesh):
    in_specs = (
        P("blk", "tp"),
        P(None, "tp"),
        P(None, "tp"),
        P(None, "tp"),
        P("tp", None),
        P("blk", "tp", None),
        P("blk", "tp", None),
        P("blk", None),
        P("blk"),
    )
    out_specs = P(("blk", "tp"), None)
    return jax.shard_map(
        per_device, mesh=mesh, in_specs=in_specs, out_specs=out_specs, check_vma=False
    )
```

```python
import functools
import math

import jax
import jax.numpy as jnp
from jax import lax
from jax.experimental import pallas as pl
from jax.experimental.pallas import tpu as pltpu
from jax.sharding import PartitionSpec as P

HD = 128
BLOCK = 512
ROPE_BASE = 1000000.0
NEGATIVE = -1e30
SCALE = math.log2(math.e) / math.sqrt(HD)

NX, NY, NC = 4, 2, 2
NL, NZ = 2, 4


def send(value, dx=0, dy=0, dc=0):
    pairs = []
    for x in range(NX):
        for y in range(NY):
            for c in range(NC):
                src = (x * NY + y) * NC + c
                dst = ((x + dx) % NX * NY + (y + dy) % NY) * NC + (c + dc) % NC
                pairs.append((src, dst))
    return lax.ppermute(value, "blk", pairs)


def send_tp(value, dl=0, dz=0):
    pairs = []
    for l in range(NL):
        for z in range(NZ):
            pairs.append((l * NZ + z, (l + dl) % NL * NZ + (z + dz) % NZ))
    return lax.ppermute(value, "tp", pairs)


def after(value, *done):
    return lax.optimization_barrier((value, *done))[0]


SMALL = pl.CostEstimate(flops=1 << 16, bytes_accessed=1 << 14, transcendentals=0)
LONG = pl.CostEstimate(flops=8 << 30, bytes_accessed=16 << 20, transcendentals=0)
VMEM = pl.BlockSpec(memory_space=pltpu.VMEM)
HBM = pl.BlockSpec(memory_space=pl.ANY)
SMEM = pl.BlockSpec(memory_space=pltpu.SMEM)
def roomy(mebibytes):
    return pltpu.CompilerParams(vmem_limit_bytes=mebibytes * 1024 * 1024)


PARAMS = pltpu.CompilerParams(vmem_limit_bytes=24 * 1024 * 1024)


WIDE, SLIM = 512, 128
PART = 1024


def weight_copies(ids, weights, out, sems, base, i):
    rows = pl.ds(pl.multiple_of(ids[base + i] * PART, PART), PART)
    low = 0
    copies = []
    for j, ref in enumerate(weights):
        width = ref.shape[1]
        copies.append(
            pltpu.make_async_copy(ref.at[rows], out.at[i, :, low : low + width], sems.at[base + i, j])
        )
        low += width
    return copies


def accumulate(ids, chunks, weights, acc, acc_in, wbuf, xbuf, sems):
    copies = []
    for i, chunk in enumerate(chunks):
        copies.append(
            weight_copies(ids, weights, wbuf, sems, 0, i)
            + [pltpu.make_async_copy(chunk, xbuf.at[i], sems.at[i, 3])]
        )
        for copy in copies[i]:
            copy.start()
    for i in range(len(chunks)):
        for copy in copies[i]:
            copy.wait()
        for low in range(0, WIDE + 2 * SLIM, 256):
            cols = pl.ds(low, 256)
            product = jnp.dot(xbuf[i], wbuf[i, :, cols], preferred_element_type=jnp.float32)
            before = acc_in if i == 0 else acc
            acc[:, cols] = product if before is None else product + before[:, cols]


BUFS = [
    pltpu.VMEM((4, PART, WIDE + 2 * SLIM), jnp.bfloat16),
    pltpu.VMEM((4, 256, PART), jnp.bfloat16),
    pltpu.SemaphoreType.DMA((4, 4)),
]


def first_kernel(ids, t0, t1, t2, t3, wq, wk, wv, acc, wbuf, xbuf, sems):
    accumulate(ids, (t0, t1, t2, t3), (wq, wk, wv), acc, None, wbuf, xbuf, sems)


def project_first(ids, chunks, weights):
    return pl.pallas_call(
        first_kernel,
        out_shape=jax.ShapeDtypeStruct((256, WIDE + 2 * SLIM), jnp.float32),
        in_specs=[SMEM] + [HBM] * 7,
        out_specs=VMEM,
        scratch_shapes=BUFS,
        compiler_params=roomy(60),
        cost_estimate=SMALL,
        name="project_first",
    )(ids, *chunks, *weights)


def last_kernel(ids, z_ref, y0_ref, y1_ref, wq, wk, wv, *rest):
    acc_in, cos_ref, sin_ref, q_ref, kv_ref, acc, wbuf, xbuf, sems = rest
    chunks = (z_ref.at[0:256], z_ref.at[256:512], y0_ref, y1_ref)
    accumulate(ids, chunks, (wq, wk, wv), acc, acc_in, wbuf, xbuf, sems)
    for s in range(2):
        rows = pl.ds(s * 128, 128)
        cosine, sine = cos_ref[rows], sin_ref[rows]

        def rope(low):
            raw = acc[rows, low : low + HD]
            return (raw * cosine + pltpu.roll(raw, HD // 2, 1) * sine).astype(jnp.bfloat16)

        for g in range(4):
            q_ref[s, g * 128 : (g + 1) * 128] = rope(g * HD)
        kv_ref[s] = rope(WIDE)
        kv_ref[2 + s] = acc[rows, WIDE + SLIM :].astype(jnp.bfloat16)


def project_last(ids, chunks, weights, acc, tables):
    return pl.pallas_call(
        last_kernel,
        out_shape=[
            jax.ShapeDtypeStruct((2, 512, HD), jnp.bfloat16),
            jax.ShapeDtypeStruct((4, 128, HD), jnp.bfloat16),
        ],
        in_specs=[SMEM] + [HBM] * 6 + [VMEM] * 3,
        out_specs=[VMEM] * 2,
        scratch_shapes=[pltpu.VMEM((256, WIDE + 2 * SLIM), jnp.float32)] + BUFS,
        compiler_params=roomy(60),
        cost_estimate=SMALL,
        name="project_last",
    )(ids, *chunks, *weights, acc, *tables)


UNITS = [(dx, dc) for dx in range(NX) for dc in range(NC)]


def fold(query, key, value, state, live=None):
    rows = query.shape[0]
    scores = lax.dot_general(
        query, key, (((1,), (1,)), ((), ())), preferred_element_type=jnp.float32
    )
    parts = [scores[:, i : i + HD] for i in range(0, scores.shape[1], HD)]
    if live is not None:
        parts = [jnp.where(live, part, NEGATIVE) for part in parts]
    peak = jnp.max(functools.reduce(jnp.maximum, parts), axis=-1, keepdims=True)
    peak = jnp.broadcast_to(peak, (rows, HD))
    if state is not None:
        peak = jnp.maximum(peak, state[0])
    weights = jnp.concatenate(
        [jnp.exp2((part - peak) * SCALE).astype(jnp.bfloat16) for part in parts], axis=1
    )
    wide = jnp.concatenate([value, jnp.ones_like(value)], axis=1)
    both = jnp.dot(weights, wide, preferred_element_type=jnp.float32)
    mixed, total = both[:, :HD], both[:, HD:]
    if state is not None:
        shrink = jnp.exp2((state[0] - peak) * SCALE)
        total = total + state[1] * shrink
        mixed = mixed + state[2] * shrink
    return peak, total, mixed


def attend_kernel(own, first, sessions, ordered, codes, q_ref, *rest):
    slots = 8 * sessions
    if own:
        kv_ref, rest = rest[0], rest[1:]
    units = {}
    rest = list(rest)
    for key in UNITS:
        if key[0] == 2:
            units[key] = (rest.pop(0).at[0], rest.pop(0).at[0])
        else:
            ref = rest.pop(0)
            units[key] = (ref.at[0], ref.at[1])
    if ordered:
        rest.pop(0)
    if own:
        out_ref, lse_ref, kbuf, vbuf, sems, m_ref, l_ref, o_ref = rest
    else:
        out_ref, kbuf, vbuf, sems, m_ref, l_ref, o_ref, stat_ref = rest

    def copies(unit, local, slot):
        rows = pl.ds(pl.multiple_of(local * BLOCK, BLOCK), BLOCK)
        return (
            pltpu.make_async_copy(units[unit][0].at[rows], kbuf.at[slot], sems.at[slot, 0]),
            pltpu.make_async_copy(units[unit][1].at[rows], vbuf.at[slot], sems.at[slot, 1]),
        )

    base = first * 8
    @pl.loop(0, slots)
    def _(slot):
        code = codes[base + slot]
        local = code & 3

        def fetch(unit):
            for copy in copies(unit, local, slot):
                copy.start()

        def pick(bit, keys):
            if len(keys) == 1:
                fetch(keys[0])
                return
            half = len(keys) // 2

            @pl.when((code & bit) != 0)
            def _():
                pick(bit // 2, keys[half:])

            @pl.when((code & bit) == 0)
            def _():
                pick(bit // 2, keys[:half])

        @pl.when(code >= 0)
        def _():
            pick(16, UNITS)

    if own:
        live = lax.broadcasted_iota(jnp.int32, (128, 128), 0) >= lax.broadcasted_iota(
            jnp.int32, (128, 128), 1
        )
        for s in range(sessions):
            for g in range(4):
                rows = pl.ds(g * 128, 128)
                m_ref[s, rows], l_ref[s, rows], o_ref[s, rows] = fold(
                    q_ref[first + s, rows], kv_ref[first + s], kv_ref[2 + first + s], None, live
                )
    else:
        m_ref[...] = jnp.full_like(m_ref, NEGATIVE)
        l_ref[...] = jnp.zeros_like(l_ref)
        o_ref[...] = jnp.zeros_like(o_ref)

    @pl.loop(0, slots)
    def _(slot):
        @pl.when(codes[base + slot] >= 0)
        def _():
            for copy in copies(UNITS[0], 0, slot):
                copy.wait()
            s = slot // 8
            for g in range(4):
                rows = pl.ds(g * 128, 128)
                state = (m_ref[s, rows], l_ref[s, rows], o_ref[s, rows])
                m_ref[s, rows], l_ref[s, rows], o_ref[s, rows] = fold(
                    q_ref[first + s, rows], kbuf[slot], vbuf[slot], state
                )

    if not own:
        stat_ref[...] = jnp.zeros_like(stat_ref)
    for s in range(sessions):
        for g in range(4):
            rows = pl.ds(g * 128, 128)
            total = l_ref[s, rows]
            if own:
                out_ref[rows] = o_ref[s, rows] / total
                lse_ref[rows] = m_ref[s, rows] * SCALE + jnp.log2(total)
            else:
                some = total > 0
                total = jnp.where(some, total, 1.0)
                at = (s * 4 + g) * 128
                out_ref[at : at + 128] = (o_ref[s, rows] / total).astype(jnp.bfloat16)
                lse = jnp.where(some, m_ref[s, rows] * SCALE + jnp.log2(total), NEGATIVE)
                stat_ref[s * 4 + g : s * 4 + g + 1] = lse.T[0:1]
    if not own:
        left = stat_ref[...]
        for i in range(3):
            part = left.astype(jnp.bfloat16)
            out_ref[1024 + i * 16 : 1040 + i * 16] = part
            left = left - part.astype(jnp.float32)


PACKED = 1024 + 48


def codes_of(lists, blk):
    owner = lists >> 2
    dx = ((owner >> 2) - (blk >> 2)) & 3
    dc = (owner ^ blk) & 1
    near = ((owner ^ blk) & 2) == 0
    return jnp.where(near, dx * 8 + dc * 4 + (lists & 3), -1).astype(jnp.int32)


def attend(codes, query, units, own=None, first=0, after=()):
    flat = []
    for key in UNITS:
        flat += list(units[key]) if key[0] == 2 else [units[key]]
    flat += after
    sessions = 2 if own is None else 1
    wide = pltpu.VMEM((sessions, 512, HD), jnp.float32)
    scratch = [
        pltpu.VMEM((8 * sessions, BLOCK, HD), jnp.bfloat16),
        pltpu.VMEM((8 * sessions, BLOCK, HD), jnp.bfloat16),
        pltpu.SemaphoreType.DMA((8 * sessions, 2)),
        wide,
        wide,
        wide,
    ]
    extra = [] if own is None else [own]
    if own is None:
        out_shape = jax.ShapeDtypeStruct((PACKED, HD), jnp.bfloat16)
        out_specs = VMEM
        scratch.append(pltpu.VMEM((16, HD), jnp.float32))
    else:
        out_shape = [jax.ShapeDtypeStruct((512, HD), jnp.float32)] * 2
        out_specs = [VMEM, VMEM]
    return pl.pallas_call(
        functools.partial(attend_kernel, own is not None, first, sessions, len(after) > 0),
        out_shape=out_shape,
        in_specs=[SMEM] + [VMEM] * (1 + len(extra)) + [HBM] * len(flat),
        out_specs=out_specs,
        scratch_shapes=scratch,
        compiler_params=PARAMS,
        cost_estimate=SMALL if own is not None and first == 0 else LONG,
        name="attend_own" if own is not None else "attend_partner",
    )(codes, query, *extra, *flat)


def combine_kernel(ids, o0_ref, lse0_ref, o1_ref, lse1_ref, back_ref, left_ref, right_ref, mix_ref):
    stats = sum(
        back_ref[1024 + i * 16 : 1040 + i * 16].astype(jnp.float32) for i in range(3)
    )
    for s, (o_ref, lse_ref) in enumerate(((o0_ref, lse0_ref), (o1_ref, lse1_ref))):
        for g in range(4):
            rows = pl.ds(g * 128, 128)
            at = s * 4 + g
            mine = lse_ref[rows]
            other = jnp.broadcast_to(stats[at : at + 1], (128, HD)).T
            top = jnp.maximum(mine, other)
            a, b = jnp.exp2(mine - top), jnp.exp2(other - top)
            back = back_ref[at * 128 : at * 128 + 128].astype(jnp.float32)
            mixed = (o_ref[rows] * a + back * b) / (a + b)
            mix_ref[s * 128 : s * 128 + 128, g * 128 : g * 128 + 128] = mixed.astype(jnp.bfloat16)
    for dl in range(NL):
        for dz in range(NZ):
            piece = mix_ref[pl.ds(pl.multiple_of(ids[dl * NZ + dz] * 32, 32), 32)]
            left_ref[(dl * NZ + dz) * 32 : (dl * NZ + dz + 1) * 32] = piece
            at = (dz + NZ - 1) % NZ * NL + dl
            right_ref[at * 32 : (at + 1) * 32] = piece


def combine(ids, own0, own1, back):
    return pl.pallas_call(
        combine_kernel,
        out_shape=[jax.ShapeDtypeStruct((256, 512), jnp.bfloat16)] * 2,
        in_specs=[SMEM] + [VMEM] * 5,
        out_specs=[VMEM, VMEM],
        scratch_shapes=[pltpu.VMEM((256, 512), jnp.bfloat16)],
        compiler_params=PARAMS,
        cost_estimate=pl.CostEstimate(flops=1 << 20, bytes_accessed=2 << 20, transcendentals=1 << 18),
        name="combine",
    )(ids, *own0, *own1, back)


def output_kernel(mix_ref, w_ref, *out_refs):
    for low in range(0, w_ref.shape[1], 256):
        cols = pl.ds(low, 256)
        product = jnp.dot(mix_ref[...], w_ref[:, cols], preferred_element_type=jnp.float32)
        at = 0
        for ref in out_refs:
            ref[:, cols] = product[at : at + ref.shape[0]].astype(jnp.bfloat16)
            at += ref.shape[0]


TILE = 512


def output(mix, w_out, start, columns, block, splits, tile=TILE):
    tile0 = start // tile
    rows = sum(splits)
    return pl.pallas_call(
        output_kernel,
        grid=(columns // tile,),
        out_shape=[jax.ShapeDtypeStruct((n, columns), jnp.bfloat16) for n in splits],
        in_specs=[
            pl.BlockSpec((rows, 512), lambda i: (block, 0)),
            pl.BlockSpec((512, tile), lambda i: (0, i + tile0)),
        ],
        out_specs=[pl.BlockSpec((n, tile), lambda i: (0, i)) for n in splits],
        compiler_params=PARAMS,
        cost_estimate=pl.CostEstimate(
            flops=2 * 256 * 512 * columns, bytes_accessed=1024 * columns, transcendentals=0
        ),
        name="output",
    )(mix, w_out)


def add(*terms):
    return sum(term.astype(jnp.float32) for term in terms).astype(jnp.bfloat16)


def project_out(ids, left, right, w_out):
    unit = w_out.shape[1] // 16
    half = unit * 7
    parts = [(half, unit * 4), (unit * 11, unit * 5)]
    r1, r2, r3 = output(right, w_out, 0, half, 0, (64, 64, 64), half // 2)
    left = after(left, r1)
    r1 = send_tp(r1, dz=1)
    r3 = send_tp(r3, dz=-1)
    r2 = send_tp(r2, dz=2)
    theres = [output(left, w_out, start, width, 1, (128,))[0] for start, width in parts]
    own_rows = after(left, *theres)
    heres = [output(own_rows, w_out, start, width, 0, (128,))[0] for start, width in parts]
    (r0,) = output(after(right, *theres), w_out, 0, half, 3, (64,), half // 2)
    theres = [send_tp(there, dl=1) for there in theres]
    r0 = after(r0, theres[0])
    along = [r0, r1, r3, r2]
    back = send_tp(add(*[v[32:] for v in along]), dl=1)
    sums = [add(*[v[:32] for v in along], back)]
    for mine, there in zip(heres, theres):
        pairs = [(mine[i * 32 : i * 32 + 32], there[i * 32 : i * 32 + 32]) for i in range(NZ)]
        l1 = send_tp(add(*pairs[1]), dz=1)
        l3 = send_tp(add(*pairs[3]), dz=-1)
        l2 = send_tp(add(*pairs[2]), dz=2)
        sums.append(add(*pairs[0], l1, l3, l2))
    return jnp.concatenate(sums, axis=1)


def rope_tables(offsets):
    half = HD // 2
    positions = offsets.astype(jnp.float32)[:, None] + jnp.arange(128, dtype=jnp.float32)[None, :]
    freqs = jnp.exp(jnp.arange(half, dtype=jnp.float32) * (-2.0 * math.log(ROPE_BASE) / HD))
    angles = positions.reshape(-1)[:, None] * freqs
    cosine, sine = jnp.cos(angles), jnp.sin(angles)
    return (
        jnp.concatenate([cosine, cosine], axis=1),
        jnp.concatenate([-sine, sine], axis=1),
    )


def per_device(
    tokens, w_query, w_key, w_value, w_out, pool_keys, pool_values, block_lists, offsets
):
    blk = lax.axis_index("blk")
    tp = lax.axis_index("tp")
    lo, z = tp // NZ, tp % NZ

    def peer(dl, dz):
        return (lo + dl) % NL * NZ + (z + dz) % NZ

    lists = block_lists.reshape(-1)
    codes = codes_of(lists, blk)
    tables = rope_tables(offsets)

    weights = (w_query, w_key, w_value)
    own = jnp.stack([pool_keys[:, 0], pool_values[:, 0]])
    t_y = send_tp(tokens, dl=1)
    t_m = send_tp(tokens, dz=1)
    t_p = send_tp(tokens, dz=-1)
    units = {(0, 0): own, (3, 0): send(own, dx=1), (1, 0): send(own, dx=-1)}
    t_y, t_m, t_p = lax.optimization_barrier((t_y, t_m, t_p))
    z_in = jnp.concatenate([tokens, t_y])
    z_two = send_tp(z_in, dz=2)
    y_m = send_tp(t_m, dl=1)
    ids = jnp.stack([peer(0, 0), peer(1, 0), peer(0, -1), peer(0, 1)])
    acc = project_first(after(ids, z_in), [tokens, t_y, t_m, t_p], weights)
    t_p, acc, *tables = lax.optimization_barrier((t_p, acc, *tables))
    y_p = send_tp(t_p, dl=1)
    far_k, far_v = after(units[3, 0], y_m)[:1], after(units[1, 0], y_m)[1:]
    units[2, 0] = (send(far_k, dx=1), send(far_v, dx=-1))
    partner_lists = send(after(lists, far_k, far_v), dy=1)
    for dx in (0, 1, 3):
        units[dx, 1] = send(after(units[dx, 0], z_two), dc=1)
    acc, partner_lists = lax.optimization_barrier((acc, partner_lists))
    partner_codes = codes_of(partner_lists, blk)
    query, pairs = project_last(
        jnp.stack([peer(0, 2), peer(1, 2), peer(1, -1), peer(1, 1)]),
        [z_two, y_m, y_p],
        weights,
        acc,
        tables,
    )
    units[2, 1] = tuple(send(after(array, query), dc=1) for array in units[2, 0])

    partner_query = send(query, dy=1)
    own0 = attend(codes, query, units, pairs, 0)
    packed = attend(partner_codes, partner_query, units, after=[own0[1]])
    back = send(packed, dy=1)
    own1 = attend(codes, query, units, pairs, 1)
    ids = jnp.stack([peer(dl, dz) for dl in range(NL) for dz in range(NZ)])
    left, right = combine(ids, own0, own1, back)
    return project_out(ids, left, right, w_out)


def solution(mesh):
    in_specs = (
        P("blk", "tp"),
        P(None, "tp"),
        P(None, "tp"),
        P(None, "tp"),
        P("tp", None),
        P("blk", "tp", None),
        P("blk", "tp", None),
        P("blk", None),
        P("blk"),
    )
    out_specs = P(("blk", "tp"), None)
    return jax.shard_map(
        per_device, mesh=mesh, in_specs=in_specs, out_specs=out_specs, check_vma=False
    )
```

```python
import functools
import math

import jax
import jax.numpy as jnp
from jax import lax
from jax.experimental import pallas as pl
from jax.experimental.pallas import tpu as pltpu
from jax.sharding import PartitionSpec as P

HD = 128
BLOCK = 512
ROPE_BASE = 1000000.0
NEGATIVE = -1e30
SCALE = math.log2(math.e) / math.sqrt(HD)

NX, NY, NC = 4, 2, 2
NL, NZ = 2, 4


def send(value, dx=0, dy=0, dc=0):
    pairs = []
    for x in range(NX):
        for y in range(NY):
            for c in range(NC):
                src = (x * NY + y) * NC + c
                dst = ((x + dx) % NX * NY + (y + dy) % NY) * NC + (c + dc) % NC
                pairs.append((src, dst))
    return lax.ppermute(value, "blk", pairs)


def send_tp(value, dl=0, dz=0):
    pairs = []
    for l in range(NL):
        for z in range(NZ):
            pairs.append((l * NZ + z, (l + dl) % NL * NZ + (z + dz) % NZ))
    return lax.ppermute(value, "tp", pairs)


def after(value, *done):
    return lax.optimization_barrier((value, *done))[0]


SMALL = pl.CostEstimate(flops=1 << 16, bytes_accessed=1 << 14, transcendentals=0)
LONG = pl.CostEstimate(flops=8 << 30, bytes_accessed=16 << 20, transcendentals=0)
VMEM = pl.BlockSpec(memory_space=pltpu.VMEM)
HBM = pl.BlockSpec(memory_space=pl.ANY)
SMEM = pl.BlockSpec(memory_space=pltpu.SMEM)
def roomy(mebibytes):
    return pltpu.CompilerParams(vmem_limit_bytes=mebibytes * 1024 * 1024)


PARAMS = pltpu.CompilerParams(vmem_limit_bytes=24 * 1024 * 1024)


WIDE, SLIM = 512, 128
PART = 1024


def weight_copies(ids, weights, out, sems, base, i):
    rows = pl.ds(pl.multiple_of(ids[base + i] * PART, PART), PART)
    low = 0
    copies = []
    for j, ref in enumerate(weights):
        width = ref.shape[1]
        copies.append(
            pltpu.make_async_copy(ref.at[rows], out.at[i, :, low : low + width], sems.at[base + i, j])
        )
        low += width
    return copies


def accumulate(ids, chunks, weights, acc, acc_in, wbuf, xbuf, sems):
    copies = []
    for i, chunk in enumerate(chunks):
        copies.append(
            weight_copies(ids, weights, wbuf, sems, 0, i)
            + [pltpu.make_async_copy(chunk, xbuf.at[i], sems.at[i, 3])]
        )
        for copy in copies[i]:
            copy.start()
    for i in range(len(chunks)):
        for copy in copies[i]:
            copy.wait()
        for low in range(0, WIDE + 2 * SLIM, 256):
            cols = pl.ds(low, 256)
            product = jnp.dot(xbuf[i], wbuf[i, :, cols], preferred_element_type=jnp.float32)
            before = acc_in if i == 0 else acc
            acc[:, cols] = product if before is None else product + before[:, cols]


BUFS = [
    pltpu.VMEM((4, PART, WIDE + 2 * SLIM), jnp.bfloat16),
    pltpu.VMEM((4, 256, PART), jnp.bfloat16),
    pltpu.SemaphoreType.DMA((4, 4)),
]


def first_kernel(ids, t0, t1, t2, t3, wq, wk, wv, acc, wbuf, xbuf, sems):
    accumulate(ids, (t0, t1, t2, t3), (wq, wk, wv), acc, None, wbuf, xbuf, sems)


def project_first(ids, chunks, weights):
    return pl.pallas_call(
        first_kernel,
        out_shape=jax.ShapeDtypeStruct((256, WIDE + 2 * SLIM), jnp.float32),
        in_specs=[SMEM] + [HBM] * 7,
        out_specs=VMEM,
        scratch_shapes=BUFS,
        compiler_params=roomy(60),
        cost_estimate=SMALL,
        name="project_first",
    )(ids, *chunks, *weights)


def last_kernel(ids, z_ref, y0_ref, y1_ref, wq, wk, wv, *rest):
    acc_in, cos_ref, sin_ref, q_ref, kv_ref, acc, wbuf, xbuf, sems = rest
    chunks = (z_ref.at[0:256], z_ref.at[256:512], y0_ref, y1_ref)
    accumulate(ids, chunks, (wq, wk, wv), acc, acc_in, wbuf, xbuf, sems)
    for s in range(2):
        rows = pl.ds(s * 128, 128)
        cosine, sine = cos_ref[rows], sin_ref[rows]

        def rope(low):
            raw = acc[rows, low : low + HD]
            return (raw * cosine + pltpu.roll(raw, HD // 2, 1) * sine).astype(jnp.bfloat16)

        for g in range(4):
            q_ref[s, g * 128 : (g + 1) * 128] = rope(g * HD)
        kv_ref[s] = rope(WIDE)
        kv_ref[2 + s] = acc[rows, WIDE + SLIM :].astype(jnp.bfloat16)


def project_last(ids, chunks, weights, acc, tables):
    return pl.pallas_call(
        last_kernel,
        out_shape=[
            jax.ShapeDtypeStruct((2, 512, HD), jnp.bfloat16),
            jax.ShapeDtypeStruct((4, 128, HD), jnp.bfloat16),
        ],
        in_specs=[SMEM] + [HBM] * 6 + [VMEM] * 3,
        out_specs=[VMEM] * 2,
        scratch_shapes=[pltpu.VMEM((256, WIDE + 2 * SLIM), jnp.float32)] + BUFS,
        compiler_params=roomy(50),
        cost_estimate=SMALL,
        name="project_last",
    )(ids, *chunks, *weights, acc, *tables)


UNITS = [(dx, dc) for dx in range(NX) for dc in range(NC)]


def fold(query, key, value, state, live=None):
    rows = query.shape[0]
    scores = lax.dot_general(
        query, key, (((1,), (1,)), ((), ())), preferred_element_type=jnp.float32
    )
    parts = [scores[:, i : i + HD] for i in range(0, scores.shape[1], HD)]
    if live is not None:
        parts = [jnp.where(live, part, NEGATIVE) for part in parts]
    peak = jnp.max(functools.reduce(jnp.maximum, parts), axis=-1, keepdims=True)
    peak = jnp.broadcast_to(peak, (rows, HD))
    if state is not None:
        peak = jnp.maximum(peak, state[0])
    weights = jnp.concatenate(
        [jnp.exp2((part - peak) * SCALE).astype(jnp.bfloat16) for part in parts], axis=1
    )
    wide = jnp.concatenate([value, jnp.ones_like(value)], axis=1)
    both = jnp.dot(weights, wide, preferred_element_type=jnp.float32)
    mixed, total = both[:, :HD], both[:, HD:]
    if state is not None:
        shrink = jnp.exp2((state[0] - peak) * SCALE)
        total = total + state[1] * shrink
        mixed = mixed + state[2] * shrink
    return peak, total, mixed


def attend_kernel(own, first, sessions, ordered, codes, q_ref, *rest):
    slots = 8 * sessions
    if own:
        kv_ref, rest = rest[0], rest[1:]
    units = {}
    rest = list(rest)
    for key in UNITS:
        if key[0] == 2:
            units[key] = (rest.pop(0).at[0], rest.pop(0).at[0])
        else:
            ref = rest.pop(0)
            units[key] = (ref.at[0], ref.at[1])
    if ordered:
        rest.pop(0)
    if own:
        out_ref, lse_ref, kbuf, vbuf, sems, m_ref, l_ref, o_ref = rest
    else:
        out_ref, kbuf, vbuf, sems, m_ref, l_ref, o_ref, stat_ref = rest

    def copies(unit, local, slot):
        rows = pl.ds(pl.multiple_of(local * BLOCK, BLOCK), BLOCK)
        return (
            pltpu.make_async_copy(units[unit][0].at[rows], kbuf.at[slot], sems.at[slot, 0]),
            pltpu.make_async_copy(units[unit][1].at[rows], vbuf.at[slot], sems.at[slot, 1]),
        )

    base = first * 8
    @pl.loop(0, slots)
    def _(slot):
        code = codes[base + slot]
        local = code & 3

        def fetch(unit):
            for copy in copies(unit, local, slot):
                copy.start()

        def pick(bit, keys):
            if len(keys) == 1:
                fetch(keys[0])
                return
            half = len(keys) // 2

            @pl.when((code & bit) != 0)
            def _():
                pick(bit // 2, keys[half:])

            @pl.when((code & bit) == 0)
            def _():
                pick(bit // 2, keys[:half])

        @pl.when(code >= 0)
        def _():
            pick(16, UNITS)

    if own:
        live = lax.broadcasted_iota(jnp.int32, (128, 128), 0) >= lax.broadcasted_iota(
            jnp.int32, (128, 128), 1
        )
        for s in range(sessions):
            for g in range(4):
                rows = pl.ds(g * 128, 128)
                m_ref[s, rows], l_ref[s, rows], o_ref[s, rows] = fold(
                    q_ref[first + s, rows], kv_ref[first + s], kv_ref[2 + first + s], None, live
                )
    else:
        m_ref[...] = jnp.full_like(m_ref, NEGATIVE)
        l_ref[...] = jnp.zeros_like(l_ref)
        o_ref[...] = jnp.zeros_like(o_ref)

    @pl.loop(0, slots)
    def _(slot):
        @pl.when(codes[base + slot] >= 0)
        def _():
            for copy in copies(UNITS[0], 0, slot):
                copy.wait()
            s = slot // 8
            for g in range(4):
                rows = pl.ds(g * 128, 128)
                state = (m_ref[s, rows], l_ref[s, rows], o_ref[s, rows])
                m_ref[s, rows], l_ref[s, rows], o_ref[s, rows] = fold(
                    q_ref[first + s, rows], kbuf[slot], vbuf[slot], state
                )

    if not own:
        stat_ref[...] = jnp.zeros_like(stat_ref)
    for s in range(sessions):
        for g in range(4):
            rows = pl.ds(g * 128, 128)
            total = l_ref[s, rows]
            if own:
                out_ref[rows] = o_ref[s, rows] / total
                lse_ref[rows] = m_ref[s, rows] * SCALE + jnp.log2(total)
            else:
                some = total > 0
                total = jnp.where(some, total, 1.0)
                at = (s * 4 + g) * 128
                out_ref[at : at + 128] = (o_ref[s, rows] / total).astype(jnp.bfloat16)
                lse = jnp.where(some, m_ref[s, rows] * SCALE + jnp.log2(total), NEGATIVE)
                stat_ref[s * 4 + g : s * 4 + g + 1] = lse.T[0:1]
    if not own:
        left = stat_ref[...]
        for i in range(3):
            part = left.astype(jnp.bfloat16)
            out_ref[1024 + i * 16 : 1040 + i * 16] = part
            left = left - part.astype(jnp.float32)


PACKED = 1024 + 48


def codes_of(lists, blk):
    owner = lists >> 2
    dx = ((owner >> 2) - (blk >> 2)) & 3
    dc = (owner ^ blk) & 1
    near = ((owner ^ blk) & 2) == 0
    return jnp.where(near, dx * 8 + dc * 4 + (lists & 3), -1).astype(jnp.int32)


def attend(codes, query, units, own=None, first=0, after=()):
    flat = []
    for key in UNITS:
        flat += list(units[key]) if key[0] == 2 else [units[key]]
    flat += after
    sessions = 2 if own is None else 1
    wide = pltpu.VMEM((sessions, 512, HD), jnp.float32)
    scratch = [
        pltpu.VMEM((8 * sessions, BLOCK, HD), jnp.bfloat16),
        pltpu.VMEM((8 * sessions, BLOCK, HD), jnp.bfloat16),
        pltpu.SemaphoreType.DMA((8 * sessions, 2)),
        wide,
        wide,
        wide,
    ]
    extra = [] if own is None else [own]
    if own is None:
        out_shape = jax.ShapeDtypeStruct((PACKED, HD), jnp.bfloat16)
        out_specs = VMEM
        scratch.append(pltpu.VMEM((16, HD), jnp.float32))
    else:
        out_shape = [jax.ShapeDtypeStruct((512, HD), jnp.float32)] * 2
        out_specs = [VMEM, VMEM]
    return pl.pallas_call(
        functools.partial(attend_kernel, own is not None, first, sessions, len(after) > 0),
        out_shape=out_shape,
        in_specs=[SMEM] + [VMEM] * (1 + len(extra)) + [HBM] * len(flat),
        out_specs=out_specs,
        scratch_shapes=scratch,
        compiler_params=PARAMS,
        cost_estimate=SMALL if own is not None and first == 0 else LONG,
        name="attend_own" if own is not None else "attend_partner",
    )(codes, query, *extra, *flat)


def combine_kernel(ids, o0_ref, lse0_ref, o1_ref, lse1_ref, back_ref, left_ref, right_ref, mix_ref):
    stats = sum(
        back_ref[1024 + i * 16 : 1040 + i * 16].astype(jnp.float32) for i in range(3)
    )
    for s, (o_ref, lse_ref) in enumerate(((o0_ref, lse0_ref), (o1_ref, lse1_ref))):
        for g in range(4):
            rows = pl.ds(g * 128, 128)
            at = s * 4 + g
            mine = lse_ref[rows]
            other = jnp.broadcast_to(stats[at : at + 1], (128, HD)).T
            top = jnp.maximum(mine, other)
            a, b = jnp.exp2(mine - top), jnp.exp2(other - top)
            back = back_ref[at * 128 : at * 128 + 128].astype(jnp.float32)
            mixed = (o_ref[rows] * a + back * b) / (a + b)
            mix_ref[s * 128 : s * 128 + 128, g * 128 : g * 128 + 128] = mixed.astype(jnp.bfloat16)
    for dl in range(NL):
        for dz in range(NZ):
            piece = mix_ref[pl.ds(pl.multiple_of(ids[dl * NZ + dz] * 32, 32), 32)]
            left_ref[(dl * NZ + dz) * 32 : (dl * NZ + dz + 1) * 32] = piece
            at = (dz + NZ - 1) % NZ * NL + dl
            right_ref[at * 32 : (at + 1) * 32] = piece


def combine(ids, own0, own1, back):
    return pl.pallas_call(
        combine_kernel,
        out_shape=[jax.ShapeDtypeStruct((256, 512), jnp.bfloat16)] * 2,
        in_specs=[SMEM] + [VMEM] * 5,
        out_specs=[VMEM, VMEM],
        scratch_shapes=[pltpu.VMEM((256, 512), jnp.bfloat16)],
        compiler_params=PARAMS,
        cost_estimate=pl.CostEstimate(flops=1 << 20, bytes_accessed=2 << 20, transcendentals=1 << 18),
        name="combine",
    )(ids, *own0, *own1, back)


def output_kernel(mix_ref, w_ref, *out_refs):
    for low in range(0, w_ref.shape[1], 256):
        cols = pl.ds(low, 256)
        product = jnp.dot(mix_ref[...], w_ref[:, cols], preferred_element_type=jnp.float32)
        at = 0
        for ref in out_refs:
            ref[:, cols] = product[at : at + ref.shape[0]].astype(jnp.bfloat16)
            at += ref.shape[0]


TILE = 512


def output(mix, w_out, start, columns, block, splits):
    tile0 = start // TILE
    rows = sum(splits)
    return pl.pallas_call(
        output_kernel,
        grid=(columns // TILE,),
        out_shape=[jax.ShapeDtypeStruct((n, columns), jnp.bfloat16) for n in splits],
        in_specs=[
            pl.BlockSpec((rows, 512), lambda i: (block, 0)),
            pl.BlockSpec((512, TILE), lambda i: (0, i + tile0)),
        ],
        out_specs=[pl.BlockSpec((n, TILE), lambda i: (0, i)) for n in splits],
        compiler_params=PARAMS,
        cost_estimate=pl.CostEstimate(
            flops=2 * 256 * 512 * columns, bytes_accessed=1024 * columns, transcendentals=0
        ),
        name="output",
    )(mix, w_out)


def add(*terms):
    return sum(term.astype(jnp.float32) for term in terms).astype(jnp.bfloat16)


def project_out(ids, left, right, w_out):
    unit = w_out.shape[1] // 16
    half = unit * 7
    parts = [(half, unit * 4), (unit * 11, unit * 5)]
    r1, r2, r3 = output(right, w_out, 0, half, 0, (64, 64, 64))
    left = after(left, r1)
    r1 = send_tp(r1, dz=1)
    r3 = send_tp(r3, dz=-1)
    r2 = send_tp(r2, dz=2)
    theres = [output(left, w_out, start, width, 1, (128,))[0] for start, width in parts]
    own_rows = after(left, *theres)
    heres = [output(own_rows, w_out, start, width, 0, (128,))[0] for start, width in parts]
    (r0,) = output(after(right, *theres), w_out, 0, half, 3, (64,))
    theres = [send_tp(there, dl=1) for there in theres]
    r0 = after(r0, theres[0])
    along = [r0, r1, r3, r2]
    back = send_tp(add(*[v[32:] for v in along]), dl=1)
    sums = [add(*[v[:32] for v in along], back)]
    for mine, there in zip(heres, theres):
        pairs = [(mine[i * 32 : i * 32 + 32], there[i * 32 : i * 32 + 32]) for i in range(NZ)]
        l1 = send_tp(add(*pairs[1]), dz=1)
        l3 = send_tp(add(*pairs[3]), dz=-1)
        l2 = send_tp(add(*pairs[2]), dz=2)
        sums.append(add(*pairs[0], l1, l3, l2))
    return jnp.concatenate(sums, axis=1)


def rope_tables(offsets):
    half = HD // 2
    positions = offsets.astype(jnp.float32)[:, None] + jnp.arange(128, dtype=jnp.float32)[None, :]
    freqs = jnp.exp(jnp.arange(half, dtype=jnp.float32) * (-2.0 * math.log(ROPE_BASE) / HD))
    angles = positions.reshape(-1)[:, None] * freqs
    cosine, sine = jnp.cos(angles), jnp.sin(angles)
    return (
        jnp.concatenate([cosine, cosine], axis=1),
        jnp.concatenate([-sine, sine], axis=1),
    )


def per_device(
    tokens, w_query, w_key, w_value, w_out, pool_keys, pool_values, block_lists, offsets
):
    blk = lax.axis_index("blk")
    tp = lax.axis_index("tp")
    lo, z = tp // NZ, tp % NZ

    def peer(dl, dz):
        return (lo + dl) % NL * NZ + (z + dz) % NZ

    lists = block_lists.reshape(-1)
    codes = codes_of(lists, blk)
    tables = rope_tables(offsets)

    weights = (w_query, w_key, w_value)
    own = jnp.stack([pool_keys[:, 0], pool_values[:, 0]])
    t_y = send_tp(tokens, dl=1)
    t_m = send_tp(tokens, dz=1)
    t_p = send_tp(tokens, dz=-1)
    units = {(0, 0): own, (3, 0): send(own, dx=1), (1, 0): send(own, dx=-1)}
    t_y, t_m, t_p = lax.optimization_barrier((t_y, t_m, t_p))
    z_in = jnp.concatenate([tokens, t_y])
    z_two = send_tp(z_in, dz=2)
    y_m = send_tp(t_m, dl=1)
    ids = jnp.stack([peer(0, 0), peer(1, 0), peer(0, -1), peer(0, 1)])
    acc = project_first(after(ids, z_in), [tokens, t_y, t_m, t_p], weights)
    t_p, acc = lax.optimization_barrier((t_p, acc))
    y_p = send_tp(t_p, dl=1)
    far_k, far_v = after(units[3, 0], y_m)[:1], after(units[1, 0], y_m)[1:]
    units[2, 0] = (send(far_k, dx=1), send(far_v, dx=-1))
    acc, partner_lists = lax.optimization_barrier((acc, send(after(lists, far_k, far_v), dy=1)))
    partner_codes = codes_of(partner_lists, blk)
    for dx in (0, 1, 3):
        units[dx, 1] = send(after(units[dx, 0], z_two), dc=1)
    query, pairs = project_last(
        jnp.stack([peer(0, 2), peer(1, 2), peer(1, -1), peer(1, 1)]),
        [z_two, y_m, y_p],
        weights,
        acc,
        tables,
    )
    units[2, 1] = tuple(send(after(array, query), dc=1) for array in units[2, 0])

    partner_query = send(query, dy=1)
    own0 = attend(codes, query, units, pairs, 0)
    packed = attend(partner_codes, partner_query, units, after=[own0[1]])
    back = send(packed, dy=1)
    own1 = attend(codes, query, units, pairs, 1)
    ids = jnp.stack([peer(dl, dz) for dl in range(NL) for dz in range(NZ)])
    left, right = combine(ids, own0, own1, back)
    return project_out(ids, left, right, w_out)


def solution(mesh):
    in_specs = (
        P("blk", "tp"),
        P(None, "tp"),
        P(None, "tp"),
        P(None, "tp"),
        P("tp", None),
        P("blk", "tp", None),
        P("blk", "tp", None),
        P("blk", None),
        P("blk"),
    )
    out_specs = P(("blk", "tp"), None)
    return jax.shard_map(
        per_device, mesh=mesh, in_specs=in_specs, out_specs=out_specs, check_vma=False
    )
```

```python
import functools
import math

import jax
import jax.numpy as jnp
from jax import lax
from jax.experimental import pallas as pl
from jax.experimental.pallas import tpu as pltpu
from jax.sharding import PartitionSpec as P

HD = 128
BLOCK = 512
ROPE_BASE = 1000000.0
NEGATIVE = -1e30
SCALE = math.log2(math.e) / math.sqrt(HD)

NX, NY, NC = 4, 2, 2
NL, NZ = 2, 4


def send(value, dx=0, dy=0, dc=0):
    pairs = []
    for x in range(NX):
        for y in range(NY):
            for c in range(NC):
                src = (x * NY + y) * NC + c
                dst = ((x + dx) % NX * NY + (y + dy) % NY) * NC + (c + dc) % NC
                pairs.append((src, dst))
    return lax.ppermute(value, "blk", pairs)


def send_tp(value, dl=0, dz=0):
    pairs = []
    for l in range(NL):
        for z in range(NZ):
            pairs.append((l * NZ + z, (l + dl) % NL * NZ + (z + dz) % NZ))
    return lax.ppermute(value, "tp", pairs)


def after(value, *done):
    return lax.optimization_barrier((value, *done))[0]


SMALL = pl.CostEstimate(flops=1 << 16, bytes_accessed=1 << 14, transcendentals=0)
LONG = pl.CostEstimate(flops=8 << 30, bytes_accessed=16 << 20, transcendentals=0)
VMEM = pl.BlockSpec(memory_space=pltpu.VMEM)
HBM = pl.BlockSpec(memory_space=pl.ANY)
SMEM = pl.BlockSpec(memory_space=pltpu.SMEM)
def roomy(mebibytes):
    return pltpu.CompilerParams(vmem_limit_bytes=mebibytes * 1024 * 1024)


PARAMS = pltpu.CompilerParams(vmem_limit_bytes=24 * 1024 * 1024)


WIDE, SLIM = 512, 128
PART = 1024


def weight_copies(ids, weights, out, sems, base, i):
    rows = pl.ds(pl.multiple_of(ids[base + i] * PART, PART), PART)
    low = 0
    copies = []
    for j, ref in enumerate(weights):
        width = ref.shape[1]
        copies.append(
            pltpu.make_async_copy(ref.at[rows], out.at[i, :, low : low + width], sems.at[base + i, j])
        )
        low += width
    return copies


def accumulate(ids, chunks, weights, acc, acc_in, wbuf, xbuf, sems):
    copies = []
    for i, chunk in enumerate(chunks):
        copies.append(
            weight_copies(ids, weights, wbuf, sems, 0, i)
            + [pltpu.make_async_copy(chunk, xbuf.at[i], sems.at[i, 3])]
        )
        for copy in copies[i]:
            copy.start()
    for i in range(len(chunks)):
        for copy in copies[i]:
            copy.wait()
        for low in range(0, WIDE + 2 * SLIM, 256):
            cols = pl.ds(low, 256)
            product = jnp.dot(xbuf[i], wbuf[i, :, cols], preferred_element_type=jnp.float32)
            before = acc_in if i == 0 else acc
            acc[:, cols] = product if before is None else product + before[:, cols]


BUFS = [
    pltpu.VMEM((4, PART, WIDE + 2 * SLIM), jnp.bfloat16),
    pltpu.VMEM((4, 256, PART), jnp.bfloat16),
    pltpu.SemaphoreType.DMA((4, 4)),
]


def first_kernel(ids, t0, t1, t2, t3, wq, wk, wv, acc, wbuf, xbuf, sems):
    accumulate(ids, (t0, t1, t2, t3), (wq, wk, wv), acc, None, wbuf, xbuf, sems)


def project_first(ids, chunks, weights):
    return pl.pallas_call(
        first_kernel,
        out_shape=jax.ShapeDtypeStruct((256, WIDE + 2 * SLIM), jnp.float32),
        in_specs=[SMEM] + [HBM] * 7,
        out_specs=VMEM,
        scratch_shapes=BUFS,
        compiler_params=roomy(60),
        cost_estimate=SMALL,
        name="project_first",
    )(ids, *chunks, *weights)


def last_kernel(ids, z_ref, y0_ref, y1_ref, wq, wk, wv, *rest):
    acc_in, cos_ref, sin_ref, q_ref, kv_ref, acc, wbuf, xbuf, sems = rest
    chunks = (z_ref.at[0:256], z_ref.at[256:512], y0_ref, y1_ref)
    accumulate(ids, chunks, (wq, wk, wv), acc, acc_in, wbuf, xbuf, sems)
    for s in range(2):
        rows = pl.ds(s * 128, 128)
        cosine, sine = cos_ref[rows], sin_ref[rows]

        def rope(low):
            raw = acc[rows, low : low + HD]
            return (raw * cosine + pltpu.roll(raw, HD // 2, 1) * sine).astype(jnp.bfloat16)

        for g in range(4):
            q_ref[s, g * 128 : (g + 1) * 128] = rope(g * HD)
        kv_ref[s] = rope(WIDE)
        kv_ref[2 + s] = acc[rows, WIDE + SLIM :].astype(jnp.bfloat16)


def project_last(ids, chunks, weights, acc, tables):
    return pl.pallas_call(
        last_kernel,
        out_shape=[
            jax.ShapeDtypeStruct((2, 512, HD), jnp.bfloat16),
            jax.ShapeDtypeStruct((4, 128, HD), jnp.bfloat16),
        ],
        in_specs=[SMEM] + [HBM] * 6 + [VMEM] * 3,
        out_specs=[VMEM] * 2,
        scratch_shapes=[pltpu.VMEM((256, WIDE + 2 * SLIM), jnp.float32)] + BUFS,
        compiler_params=roomy(50),
        cost_estimate=SMALL,
        name="project_last",
    )(ids, *chunks, *weights, acc, *tables)


UNITS = [(dx, dc) for dx in range(NX) for dc in range(NC)]


def fold(query, key, value, state, live=None):
    rows = query.shape[0]
    scores = lax.dot_general(
        query, key, (((1,), (1,)), ((), ())), preferred_element_type=jnp.float32
    )
    parts = [scores[:, i : i + HD] for i in range(0, scores.shape[1], HD)]
    if live is not None:
        parts = [jnp.where(live, part, NEGATIVE) for part in parts]
    peak = jnp.max(functools.reduce(jnp.maximum, parts), axis=-1, keepdims=True)
    peak = jnp.broadcast_to(peak, (rows, HD))
    if state is not None:
        peak = jnp.maximum(peak, state[0])
    weights = jnp.concatenate(
        [jnp.exp2((part - peak) * SCALE).astype(jnp.bfloat16) for part in parts], axis=1
    )
    wide = jnp.concatenate([value, jnp.ones_like(value)], axis=1)
    both = jnp.dot(weights, wide, preferred_element_type=jnp.float32)
    mixed, total = both[:, :HD], both[:, HD:]
    if state is not None:
        shrink = jnp.exp2((state[0] - peak) * SCALE)
        total = total + state[1] * shrink
        mixed = mixed + state[2] * shrink
    return peak, total, mixed


def attend_kernel(own, first, sessions, ordered, codes, q_ref, *rest):
    slots = 8 * sessions
    if own:
        kv_ref, rest = rest[0], rest[1:]
    units = {}
    rest = list(rest)
    for key in UNITS:
        if key[0] == 2:
            units[key] = (rest.pop(0).at[0], rest.pop(0).at[0])
        else:
            ref = rest.pop(0)
            units[key] = (ref.at[0], ref.at[1])
    if ordered:
        rest.pop(0)
    if own:
        out_ref, lse_ref, kbuf, vbuf, sems, m_ref, l_ref, o_ref = rest
    else:
        out_ref, kbuf, vbuf, sems, m_ref, l_ref, o_ref, stat_ref = rest

    def copies(unit, local, slot):
        rows = pl.ds(pl.multiple_of(local * BLOCK, BLOCK), BLOCK)
        return (
            pltpu.make_async_copy(units[unit][0].at[rows], kbuf.at[slot], sems.at[slot, 0]),
            pltpu.make_async_copy(units[unit][1].at[rows], vbuf.at[slot], sems.at[slot, 1]),
        )

    base = first * 8
    @pl.loop(0, slots)
    def _(slot):
        code = codes[base + slot]
        local = code & 3

        def fetch(unit):
            for copy in copies(unit, local, slot):
                copy.start()

        def pick(bit, keys):
            if len(keys) == 1:
                fetch(keys[0])
                return
            half = len(keys) // 2

            @pl.when((code & bit) != 0)
            def _():
                pick(bit // 2, keys[half:])

            @pl.when((code & bit) == 0)
            def _():
                pick(bit // 2, keys[:half])

        @pl.when(code >= 0)
        def _():
            pick(16, UNITS)

    if own:
        live = lax.broadcasted_iota(jnp.int32, (128, 128), 0) >= lax.broadcasted_iota(
            jnp.int32, (128, 128), 1
        )
        for s in range(sessions):
            for g in range(4):
                rows = pl.ds(g * 128, 128)
                m_ref[s, rows], l_ref[s, rows], o_ref[s, rows] = fold(
                    q_ref[first + s, rows], kv_ref[first + s], kv_ref[2 + first + s], None, live
                )
    else:
        m_ref[...] = jnp.full_like(m_ref, NEGATIVE)
        l_ref[...] = jnp.zeros_like(l_ref)
        o_ref[...] = jnp.zeros_like(o_ref)

    @pl.loop(0, slots)
    def _(slot):
        @pl.when(codes[base + slot] >= 0)
        def _():
            for copy in copies(UNITS[0], 0, slot):
                copy.wait()
            s = slot // 8
            for g in range(4):
                rows = pl.ds(g * 128, 128)
                state = (m_ref[s, rows], l_ref[s, rows], o_ref[s, rows])
                m_ref[s, rows], l_ref[s, rows], o_ref[s, rows] = fold(
                    q_ref[first + s, rows], kbuf[slot], vbuf[slot], state
                )

    if not own:
        stat_ref[...] = jnp.zeros_like(stat_ref)
    for s in range(sessions):
        for g in range(4):
            rows = pl.ds(g * 128, 128)
            total = l_ref[s, rows]
            if own:
                out_ref[rows] = o_ref[s, rows] / total
                lse_ref[rows] = m_ref[s, rows] * SCALE + jnp.log2(total)
            else:
                some = total > 0
                total = jnp.where(some, total, 1.0)
                at = (s * 4 + g) * 128
                out_ref[at : at + 128] = (o_ref[s, rows] / total).astype(jnp.bfloat16)
                lse = jnp.where(some, m_ref[s, rows] * SCALE + jnp.log2(total), NEGATIVE)
                stat_ref[s * 4 + g : s * 4 + g + 1] = lse.T[0:1]
    if not own:
        left = stat_ref[...]
        for i in range(3):
            part = left.astype(jnp.bfloat16)
            out_ref[1024 + i * 16 : 1040 + i * 16] = part
            left = left - part.astype(jnp.float32)


PACKED = 1024 + 48


def codes_of(lists, blk):
    owner = lists >> 2
    dx = ((owner >> 2) - (blk >> 2)) & 3
    dc = (owner ^ blk) & 1
    near = ((owner ^ blk) & 2) == 0
    return jnp.where(near, dx * 8 + dc * 4 + (lists & 3), -1).astype(jnp.int32)


def attend(codes, query, units, own=None, first=0, after=()):
    flat = []
    for key in UNITS:
        flat += list(units[key]) if key[0] == 2 else [units[key]]
    flat += after
    sessions = 2 if own is None else 1
    wide = pltpu.VMEM((sessions, 512, HD), jnp.float32)
    scratch = [
        pltpu.VMEM((8 * sessions, BLOCK, HD), jnp.bfloat16),
        pltpu.VMEM((8 * sessions, BLOCK, HD), jnp.bfloat16),
        pltpu.SemaphoreType.DMA((8 * sessions, 2)),
        wide,
        wide,
        wide,
    ]
    extra = [] if own is None else [own]
    if own is None:
        out_shape = jax.ShapeDtypeStruct((PACKED, HD), jnp.bfloat16)
        out_specs = VMEM
        scratch.append(pltpu.VMEM((16, HD), jnp.float32))
    else:
        out_shape = [jax.ShapeDtypeStruct((512, HD), jnp.float32)] * 2
        out_specs = [VMEM, VMEM]
    return pl.pallas_call(
        functools.partial(attend_kernel, own is not None, first, sessions, len(after) > 0),
        out_shape=out_shape,
        in_specs=[SMEM] + [VMEM] * (1 + len(extra)) + [HBM] * len(flat),
        out_specs=out_specs,
        scratch_shapes=scratch,
        compiler_params=PARAMS,
        cost_estimate=SMALL if own is not None and first == 0 else LONG,
        name="attend_own" if own is not None else "attend_partner",
    )(codes, query, *extra, *flat)


def combine_kernel(ids, o0_ref, lse0_ref, o1_ref, lse1_ref, back_ref, left_ref, right_ref, mix_ref):
    stats = sum(
        back_ref[1024 + i * 16 : 1040 + i * 16].astype(jnp.float32) for i in range(3)
    )
    for s, (o_ref, lse_ref) in enumerate(((o0_ref, lse0_ref), (o1_ref, lse1_ref))):
        for g in range(4):
            rows = pl.ds(g * 128, 128)
            at = s * 4 + g
            mine = lse_ref[rows]
            other = jnp.broadcast_to(stats[at : at + 1], (128, HD)).T
            top = jnp.maximum(mine, other)
            a, b = jnp.exp2(mine - top), jnp.exp2(other - top)
            back = back_ref[at * 128 : at * 128 + 128].astype(jnp.float32)
            mixed = (o_ref[rows] * a + back * b) / (a + b)
            mix_ref[s * 128 : s * 128 + 128, g * 128 : g * 128 + 128] = mixed.astype(jnp.bfloat16)
    for dl in range(NL):
        for dz in range(NZ):
            piece = mix_ref[pl.ds(pl.multiple_of(ids[dl * NZ + dz] * 32, 32), 32)]
            left_ref[(dl * NZ + dz) * 32 : (dl * NZ + dz + 1) * 32] = piece
            at = (dz + NZ - 1) % NZ * NL + dl
            right_ref[at * 32 : (at + 1) * 32] = piece


def combine(ids, own0, own1, back):
    return pl.pallas_call(
        combine_kernel,
        out_shape=[jax.ShapeDtypeStruct((256, 512), jnp.bfloat16)] * 2,
        in_specs=[SMEM] + [VMEM] * 5,
        out_specs=[VMEM, VMEM],
        scratch_shapes=[pltpu.VMEM((256, 512), jnp.bfloat16)],
        compiler_params=PARAMS,
        cost_estimate=pl.CostEstimate(flops=1 << 20, bytes_accessed=2 << 20, transcendentals=1 << 18),
        name="combine",
    )(ids, *own0, *own1, back)


def output_kernel(mix_ref, w_ref, *out_refs):
    for low in range(0, w_ref.shape[1], 256):
        cols = pl.ds(low, 256)
        product = jnp.dot(mix_ref[...], w_ref[:, cols], preferred_element_type=jnp.float32)
        at = 0
        for ref in out_refs:
            ref[:, cols] = product[at : at + ref.shape[0]].astype(jnp.bfloat16)
            at += ref.shape[0]


TILE = 512


def output(mix, w_out, start, columns, block, splits, tile=TILE):
    tile0 = start // tile
    rows = sum(splits)
    return pl.pallas_call(
        output_kernel,
        grid=(columns // tile,),
        out_shape=[jax.ShapeDtypeStruct((n, columns), jnp.bfloat16) for n in splits],
        in_specs=[
            pl.BlockSpec((rows, 512), lambda i: (block, 0)),
            pl.BlockSpec((512, tile), lambda i: (0, i + tile0)),
        ],
        out_specs=[pl.BlockSpec((n, tile), lambda i: (0, i)) for n in splits],
        compiler_params=PARAMS,
        cost_estimate=pl.CostEstimate(
            flops=2 * 256 * 512 * columns, bytes_accessed=1024 * columns, transcendentals=0
        ),
        name="output",
    )(mix, w_out)


def add(*terms):
    return sum(term.astype(jnp.float32) for term in terms).astype(jnp.bfloat16)


def project_out(ids, left, right, w_out):
    unit = w_out.shape[1] // 16
    half = unit * 7
    parts = [(half, unit * 4), (unit * 11, unit * 5)]
    r1, r2, r3 = output(right, w_out, 0, half, 0, (64, 64, 64), half // 2)
    left = after(left, r1)
    r1 = send_tp(r1, dz=1)
    r3 = send_tp(r3, dz=-1)
    r2 = send_tp(r2, dz=2)
    theres = [output(left, w_out, start, width, 1, (128,))[0] for start, width in parts]
    own_rows = after(left, *theres)
    heres = [output(own_rows, w_out, start, width, 0, (128,))[0] for start, width in parts]
    (r0,) = output(after(right, *theres), w_out, 0, half, 3, (64,))
    theres = [send_tp(there, dl=1) for there in theres]
    r0 = after(r0, theres[0])
    along = [r0, r1, r3, r2]
    back = send_tp(add(*[v[32:] for v in along]), dl=1)
    sums = [add(*[v[:32] for v in along], back)]
    for mine, there in zip(heres, theres):
        pairs = [(mine[i * 32 : i * 32 + 32], there[i * 32 : i * 32 + 32]) for i in range(NZ)]
        l1 = send_tp(add(*pairs[1]), dz=1)
        l3 = send_tp(add(*pairs[3]), dz=-1)
        l2 = send_tp(add(*pairs[2]), dz=2)
        sums.append(add(*pairs[0], l1, l3, l2))
    return jnp.concatenate(sums, axis=1)


def rope_tables(offsets):
    half = HD // 2
    positions = offsets.astype(jnp.float32)[:, None] + jnp.arange(128, dtype=jnp.float32)[None, :]
    freqs = jnp.exp(jnp.arange(half, dtype=jnp.float32) * (-2.0 * math.log(ROPE_BASE) / HD))
    angles = positions.reshape(-1)[:, None] * freqs
    cosine, sine = jnp.cos(angles), jnp.sin(angles)
    return (
        jnp.concatenate([cosine, cosine], axis=1),
        jnp.concatenate([-sine, sine], axis=1),
    )


def per_device(
    tokens, w_query, w_key, w_value, w_out, pool_keys, pool_values, block_lists, offsets
):
    blk = lax.axis_index("blk")
    tp = lax.axis_index("tp")
    lo, z = tp // NZ, tp % NZ

    def peer(dl, dz):
        return (lo + dl) % NL * NZ + (z + dz) % NZ

    lists = block_lists.reshape(-1)
    codes = codes_of(lists, blk)
    tables = rope_tables(offsets)

    weights = (w_query, w_key, w_value)
    own = jnp.stack([pool_keys[:, 0], pool_values[:, 0]])
    t_y = send_tp(tokens, dl=1)
    t_m = send_tp(tokens, dz=1)
    t_p = send_tp(tokens, dz=-1)
    units = {(0, 0): own, (3, 0): send(own, dx=1), (1, 0): send(own, dx=-1)}
    t_y, t_m, t_p = lax.optimization_barrier((t_y, t_m, t_p))
    z_in = jnp.concatenate([tokens, t_y])
    z_two = send_tp(z_in, dz=2)
    y_m = send_tp(t_m, dl=1)
    ids = jnp.stack([peer(0, 0), peer(1, 0), peer(0, -1), peer(0, 1)])
    acc = project_first(after(ids, z_in), [tokens, t_y, t_m, t_p], weights)
    t_p, acc = lax.optimization_barrier((t_p, acc))
    y_p = send_tp(t_p, dl=1)
    far_k, far_v = after(units[3, 0], y_m)[:1], after(units[1, 0], y_m)[1:]
    units[2, 0] = (send(far_k, dx=1), send(far_v, dx=-1))
    acc, partner_lists = lax.optimization_barrier((acc, send(after(lists, far_k, far_v), dy=1)))
    partner_codes = codes_of(partner_lists, blk)
    for dx in (0, 1, 3):
        units[dx, 1] = send(after(units[dx, 0], z_two), dc=1)
    query, pairs = project_last(
        jnp.stack([peer(0, 2), peer(1, 2), peer(1, -1), peer(1, 1)]),
        [z_two, y_m, y_p],
        weights,
        acc,
        tables,
    )
    units[2, 1] = tuple(send(after(array, query), dc=1) for array in units[2, 0])

    partner_query = send(query, dy=1)
    own0 = attend(codes, query, units, pairs, 0)
    packed = attend(partner_codes, partner_query, units, after=[own0[1]])
    back = send(packed, dy=1)
    own1 = attend(codes, query, units, pairs, 1)
    ids = jnp.stack([peer(dl, dz) for dl in range(NL) for dz in range(NZ)])
    left, right = combine(ids, own0, own1, back)
    return project_out(ids, left, right, w_out)


def solution(mesh):
    in_specs = (
        P("blk", "tp"),
        P(None, "tp"),
        P(None, "tp"),
        P(None, "tp"),
        P("tp", None),
        P("blk", "tp", None),
        P("blk", "tp", None),
        P("blk", None),
        P("blk"),
    )
    out_specs = P(("blk", "tp"), None)
    return jax.shard_map(
        per_device, mesh=mesh, in_specs=in_specs, out_specs=out_specs, check_vma=False
    )
```
